256 devices in a mesh: blk: 32 (over z, y_hi, core), uly: 8 (over x, y_lo).
Axes of the slice: x: 4, y: 4 (y_hi: 2, y_lo: 2; y = y_hi * 2 + y_lo), z: 8, core: 2. Of those that a mesh axis runs over, the one named last changes fastest.
Arguments:
- frames: bfloat16 [256, 64, 1152], P('blk', 'uly'), may hold values from -6 to 6
- vis_gain: float32 [1152], replicated, may hold values from 0.25 to 1.75
- proj_weight: bfloat16 [1152, 3584], P(None, 'uly'), may hold values from -0.1875 to 0.1875
- text_embed: bfloat16 [16384, 3584], P('blk', 'uly'), may hold values from -6 to 6
- text_lengths: int32 [32, 5], P('blk'), may hold values from 1 to 256, 512 in all within a row
- norm_gain: float32 [3584], P('uly'), may hold values from 0.25 to 1.75
- q_weight: bfloat16 [3584, 2048], P('uly'), as said below
- k_weight: bfloat16 [3584, 512], P('uly'), as said below
- v_weight: bfloat16 [3584, 512], P('uly'), may hold values from -0.09375 to 0.09375
- q_bias: float32 [2048], replicated, may hold values from -4 to 4
- k_bias: float32 [512], replicated, may hold values from -4 to 4
- v_bias: float32 [512], replicated, may hold values from -4 to 4
Outputs:
- attended: bfloat16 [24576, 2048], P('blk', 'uly')
The draws below stay inside these ranges and needn't reach their ends.
Inputs may be any that keep to these rules, and one draw needn't show every extreme that they name: `text_lengths`: row b gives the lengths of the text runs of group b, the first before its first pooled frame and the last after its last; each row sums to 512. `q_weight`: entries of order 3584 ** -0.5. `k_weight`: entries of order 3584 ** -0.5.
All inputs are finite; a program needn't handle non-finite values.
Results may differ from the reference program's by a relative error of at most 0.006.
Values may be sent and summed in bfloat16 or wider, within the bound.
A program may use at most 64 MiB of HBM per device.

```python
import math
from functools import partial
import jax
import jax.numpy as jnp
import numpy as np
from jax import lax

V = 1152
PATCH = 64
D = 3584
HQ = 16
KVH = 4
HD = 128
GRP = 768
POOL_GRP = 4
VIS_GRP = 256
TEXT_GRP = 512
FRAMES = 256
SEQ = 24576
TEXT = 16384
QPK = 4
N_BLK = 32


def shared_keys(key):
    return jax.random.normal(key, (D, KVH * HD), jnp.float32)


def draw_k_weight(key, part):
    base_rows = shared_keys(key)
    return (base_rows * (1.6 / math.sqrt(D))).astype(jnp.bfloat16)


def draw_q_weight(key, part):
    key = jax.random.fold_in(key, 11)
    fresh_rows = jax.random.normal(key, (D, HQ * HD), jnp.float32)
    combined = fresh_rows
    return (combined * (1.6 / math.sqrt(D))).astype(jnp.bfloat16)


def shard_levels(own_key, shape, cuts, least, largest):
    factor_of = 1.0
    for axis_at, blocks in cuts:
        heights = jax.random.uniform(jax.random.fold_in(jax.random.fold_in(own_key, 6), axis_at), (blocks,), jnp.float32, least / len(cuts), largest / len(cuts))
        factor_of = factor_of * jnp.repeat(jnp.exp(heights), shape[axis_at] // blocks).reshape((-1,) + (1,) * (len(shape) - 1 - axis_at))
    return factor_of


def length_profile(number_of, total, bound, skew):
    portions = [(1 << 20) // math.isqrt(standing ** skew) + 1 for standing in range(2, number_of + 1)]
    spare, holding = total - bound - (number_of - 1), [1] * (number_of - 1)
    while spare > 0:
        free = [i for i in range(number_of - 1) if holding[i] < bound]
        whole, budget = sum([portions[i] for i in free]), spare
        for i in free:
            extra = min(bound - holding[i], max(1, budget * portions[i] // whole), spare)
            holding[i] = holding[i] + extra
            spare = spare - extra
    return np.array([bound] + holding)


def uneven(stream_key, number_of, total, bound, lean):
    if number_of == 2:
        one = jax.random.randint(stream_key, (), max(1, total - bound), min(bound, total - 1) + 1)
        return jnp.stack([one, total - one])
    lengths = jnp.asarray(length_profile(number_of, total, bound, lean), jnp.int32)
    twos = (number_of - 1) // 2
    giver, sink = lengths[1:1 + 2 * twos:2], lengths[2:2 + 2 * twos:2]
    margin = jnp.minimum(giver - 1, bound - sink)
    shifted = jax.random.randint(jax.random.fold_in(stream_key, 1), (twos,), 0, 1 << 20) % (margin + 1)
    lengths = lengths.at[1:1 + 2 * twos:2].set(giver - shifted).at[2:2 + 2 * twos:2].set(sink + shifted)
    return lengths[jax.random.permutation(jax.random.fold_in(stream_key, 2), number_of)]


def scatter_about(own_key, dims, scale, most, split=(), kind=jnp.bfloat16):
    array = scale * jax.random.normal(own_key, dims, jnp.float32)
    if split:
        array = array * shard_levels(own_key, dims, split, -0.22, 0.18)
    return jnp.clip(array, -most, most).astype(kind)


def setup_inputs(seed: int = 0) -> dict:
    seeds = jax.random.split(jax.random.key(seed), 13)
    return {
        "frames": scatter_about(seeds[0], (FRAMES, PATCH, V), 1.0, 6.0, ((0, 32), (1, 8))),
        "vis_gain": jnp.clip(1.0 + 0.15 * jax.random.normal(seeds[1], (V,), jnp.float32), 0.25, 1.75),
        "proj_weight": scatter_about(seeds[2], (V, D), V ** -0.5, 0.1875, ((1, 8),)),
        "text_embed": scatter_about(seeds[3], (TEXT, D), 1.0, 6.0, ((0, 32), (1, 8))),
        "text_lengths": jax.vmap(lambda own: uneven(own, POOL_GRP + 1, TEXT_GRP, TEXT_GRP // 2, 2))(jax.random.split(seeds[4], N_BLK)).reshape((N_BLK, POOL_GRP + 1)).astype(jnp.int32),
        "norm_gain": jnp.clip(1.0 + 0.15 * jax.random.normal(seeds[5], (D,), jnp.float32), 0.25, 1.75),
        "q_weight": draw_q_weight(jax.random.fold_in(seeds[12], 71), 0),
        "k_weight": draw_k_weight(jax.random.fold_in(seeds[12], 71), 0),
        "v_weight": scatter_about(seeds[8], (D, KVH * HD), D ** -0.5, 0.09375, ((0, 8),)),
        "q_bias": scatter_about(seeds[9], (HQ * HD,), 1.0, 4.0, (), jnp.float32),
        "k_bias": scatter_about(seeds[10], (KVH * HD,), 1.0, 4.0, (), jnp.float32),
        "v_bias": scatter_about(seeds[11], (KVH * HD,), 1.0, 4.0, (), jnp.float32),
    }


def pool_frames(frames, tail_frames):
    extended = jnp.concatenate([frames, tail_frames], 0).astype(jnp.float32)
    paired_frame_sums = extended.reshape((extended.shape[0] // 2, 2) + extended.shape[1:]).sum(1)
    return (paired_frame_sums[:-1] + paired_frame_sums[1:]) * 0.25

def layer_norm(values_in, gain_vec):
    average = lax.optimization_barrier(jnp.mean(values_in, -1, keepdims=True))
    centred = values_in - average
    variance = lax.optimization_barrier(jnp.mean(centred * centred, -1, keepdims=True))
    return centred * lax.rsqrt(variance + 1e-06) * gain_vec

def alternate(vis_rows, text_rows, run_lengths, patch_len):
    frame_count = run_lengths.shape[0] - 1
    seq_total = vis_rows.shape[0] + text_rows.shape[0]
    run_ends = jnp.cumsum(run_lengths[:frame_count]).astype(jnp.int32)
    starts = run_ends + patch_len * jnp.arange(frame_count, dtype=jnp.int32)
    positions = jnp.arange(seq_total, dtype=jnp.int32)[:, None]
    inside = (positions >= starts[None]) & (positions < starts[None] + patch_len)
    before = (positions >= starts[None] + patch_len).astype(jnp.int32)
    frame_ids = jnp.arange(frame_count, dtype=jnp.int32)[None]
    vis_index = lax.optimization_barrier(jnp.sum(jnp.where(inside, frame_ids * patch_len + positions - starts[None], 0), 1)).astype(jnp.int32)
    text_index = jnp.clip(positions[:, 0] - patch_len * lax.optimization_barrier(jnp.sum(before, 1)), 0, text_rows.shape[0] - 1).astype(jnp.int32)
    in_vision = jnp.any(inside, 1)
    return jnp.where(in_vision[:, None], jnp.take(vis_rows, vis_index, 0), jnp.take(text_rows, text_index, 0))

def rotate(vectors, positions):
    half_dim = vectors.shape[-1] // 2
    inv_freq = jnp.power(jnp.float32(1000000.0), -jnp.arange(half_dim, dtype=jnp.float32) * (2.0 / vectors.shape[-1]))
    angles = positions.astype(jnp.float32)[:, None] * inv_freq[None]
    cosine = jnp.cos(angles)[:, None, :]
    sine = jnp.sin(angles)[:, None, :]
    first = vectors[..., :half_dim]
    second = vectors[..., half_dim:]
    return jnp.concatenate([first * cosine - second * sine, second * cosine + first * sine], -1)

def reference(frames, vis_gain, proj_weight, text_embed, text_lengths, norm_gain, q_weight, k_weight, v_weight, q_bias, k_bias, v_bias):
    pooled = pool_frames(frames, jnp.zeros((2,) + frames.shape[1:], frames.dtype))
    normal_vis = layer_norm(pooled, vis_gain).astype(jnp.bfloat16)
    vis_rows = jnp.dot(normal_vis.reshape(-1, V), proj_weight, preferred_element_type=jnp.float32).astype(jnp.bfloat16)
    grouped_vis = vis_rows.reshape(N_BLK, VIS_GRP, D)
    grouped_text = text_embed.reshape(N_BLK, TEXT_GRP, D)
    sequence = jax.vmap(partial(alternate, patch_len=PATCH))(grouped_vis, grouped_text, text_lengths).reshape(SEQ, D)
    seq_float = sequence.astype(jnp.float32)
    mean_sq = lax.optimization_barrier(jnp.mean(seq_float * seq_float, 1, keepdims=True))
    normalized_rows = (seq_float * lax.rsqrt(mean_sq + 1e-06) * norm_gain).astype(jnp.bfloat16)
    proj_q = jnp.dot(normalized_rows, q_weight, preferred_element_type=jnp.float32) + q_bias
    proj_k = jnp.dot(normalized_rows, k_weight, preferred_element_type=jnp.float32) + k_bias
    proj_v = jnp.dot(normalized_rows, v_weight, preferred_element_type=jnp.float32) + v_bias
    positions = jnp.arange(SEQ, dtype=jnp.int32)
    queries = rotate(proj_q.reshape(SEQ, HQ, HD), positions).astype(jnp.bfloat16)
    keys = rotate(proj_k.reshape(SEQ, KVH, HD), positions).astype(jnp.bfloat16)
    values = proj_v.reshape(SEQ, KVH, HD).astype(jnp.bfloat16)

    def one_block(block_id):
        q_rows = lax.dynamic_slice_in_dim(queries, block_id * GRP, GRP, 0)
        q_positions = block_id * GRP + jnp.arange(GRP, dtype=jnp.int32)

        def one_group(group_id):
            q_group = lax.dynamic_slice_in_dim(q_rows, group_id * QPK, QPK, 1).astype(jnp.float32)
            k_group = lax.dynamic_index_in_dim(keys, group_id, 1, keepdims=False).astype(jnp.float32)
            v_group = lax.dynamic_index_in_dim(values, group_id, 1, keepdims=False).astype(jnp.float32)
            scores = jnp.einsum('qhd,kd->hqk', q_group, k_group) / math.sqrt(HD)
            allowed = positions[None, None, :] <= q_positions[None, :, None]
            top_score = lax.optimization_barrier(jnp.max(jnp.where(allowed, scores, -1e+30), -1, keepdims=True))
            weights = jnp.where(allowed, jnp.exp(scores - top_score), 0.0)
            denoms = lax.optimization_barrier(jnp.sum(weights, -1))
            rounded_values = lax.optimization_barrier(weights.astype(jnp.bfloat16)).astype(jnp.float32)
            combined = jnp.einsum('hqk,kd->qhd', rounded_values, v_group)
            return combined / jnp.transpose(denoms)[:, :, None]
        group_outs = lax.map(one_group, jnp.arange(KVH, dtype=jnp.int32))
        return jnp.transpose(group_outs, (1, 0, 2, 3)).reshape(GRP, HQ * HD)
    blocks = lax.map(one_block, jnp.arange(N_BLK, dtype=jnp.int32))
    return blocks.reshape(SEQ, HQ * HD).astype(jnp.bfloat16)
```

```python
import functools
import math

import jax
import jax.numpy as jnp
from jax import lax
from jax.experimental import pallas as pl
from jax.experimental.pallas import tpu as pltpu
from jax.sharding import PartitionSpec as P

PATCH = 64
D = 3584
HQ = 16
KVH = 4
HD = 128
GRP = 768
ROWS = 256
EXP2_SCALE = math.log2(math.e) / math.sqrt(HD)
NEG = -1e30
MESH = pl.DeviceIdType.MESH

NZ = 8
NY = 4


def from_behind(value, axis, steps):
    count = lax.axis_size(axis)
    first, last = (max(0, -steps), min(count, count - steps))
    return lax.ppermute(value, axis, [(source, source + steps) for source in range(first, last)])


def pool_frames(frames, tail_frames):
    extended = jnp.concatenate([frames, tail_frames], 0).astype(jnp.float32)
    paired_frame_sums = extended.reshape((extended.shape[0] // 2, 2) + extended.shape[1:]).sum(1)
    return (paired_frame_sums[:-1] + paired_frame_sums[1:]) * 0.25


def layer_norm(values_in, gain_vec):
    average = jnp.mean(values_in, -1, keepdims=True)
    centred = values_in - average
    variance = jnp.mean(centred * centred, -1, keepdims=True)
    return centred * lax.rsqrt(variance + 1e-06) * gain_vec


def alternate(vis_rows, text_rows, run_lengths, patch_len):
    frame_count = run_lengths.shape[0] - 1
    seq_total = vis_rows.shape[0] + text_rows.shape[0]
    run_ends = jnp.cumsum(run_lengths[:frame_count])
    starts = run_ends + patch_len * jnp.arange(frame_count, dtype=jnp.int32)
    positions = jnp.arange(seq_total, dtype=jnp.int32)[:, None]
    inside = (positions >= starts[None]) & (positions < starts[None] + patch_len)
    before = (positions >= starts[None] + patch_len).astype(jnp.int32)
    frame_ids = jnp.arange(frame_count, dtype=jnp.int32)[None]
    vis_index = jnp.sum(jnp.where(inside, frame_ids * patch_len + positions - starts[None], 0), 1)
    text_index = jnp.clip(
        positions[:, 0] - patch_len * jnp.sum(before, 1), 0, text_rows.shape[0] - 1
    )
    in_vision = jnp.any(inside, 1)
    return jnp.where(
        in_vision[:, None], jnp.take(vis_rows, vis_index, 0), jnp.take(text_rows, text_index, 0)
    )


def rotate(vectors, angles):
    half_dim = vectors.shape[-1] // 2
    cosine = jnp.cos(angles)[:, None, :]
    sine = jnp.sin(angles)[:, None, :]
    first = vectors[..., :half_dim]
    second = vectors[..., half_dim:]
    return jnp.concatenate([first * cosine - second * sine, second * cosine + first * sine], -1)


def attention_kernel(q_ref, piece_ref, out_ref, slots, top, accum, send_sem, recv_sem):
    blk = lax.axis_index("blk")
    uly = lax.axis_index("uly")
    z, place = lax.div(blk, 4), lax.rem(blk, 4)
    y_hi, core = lax.div(place, 2), lax.rem(place, 2)
    x, y_lo = lax.div(uly, 2), lax.rem(uly, 2)
    y = 2 * y_hi + y_lo

    def device(z_at, y_at, core_at):
        return (z_at * 4 + lax.div(y_at, 2) * 2 + core_at, x * 2 + lax.rem(y_at, 2))

    z_up = device(lax.rem(z + 1, NZ), y, core)
    z_down = device(lax.rem(z + NZ - 1, NZ), y, core)
    y_up = device(z, lax.rem(y + 1, NY), core)
    y_down = device(z, lax.rem(y + NY - 1, NY), core)
    sibling = device(z, y, 1 - core)

    def slot(stage, far, other):
        return stage * 8 + far * 2 + other

    def send(source, target, sem, to):
        pltpu.make_async_remote_copy(
            src_ref=slots.at[source],
            dst_ref=slots.at[target],
            send_sem=send_sem.at[sem],
            recv_sem=recv_sem.at[target],
            device_id=to,
            device_id_type=MESH,
        ).start()

    def arrived(target):
        pltpu.make_async_remote_copy(
            src_ref=slots.at[target],
            dst_ref=slots.at[target],
            send_sem=send_sem.at[target],
            recv_sem=recv_sem.at[target],
            device_id=sibling,
            device_id_type=MESH,
        ).wait_recv()

    def sent(sem):
        pltpu.make_async_remote_copy(
            src_ref=slots.at[0],
            dst_ref=slots.at[0],
            send_sem=send_sem.at[sem],
            recv_sem=recv_sem.at[0],
            device_id=sibling,
            device_id_type=MESH,
        ).wait_send()

    def spread(stage):
        mine = slot(stage, 0, 0)
        send(mine, slot(stage, 1, 0), stage * 8 + 1, y_up)
        send(mine, slot(stage, 3, 0), stage * 8 + 2, y_down)
        send(mine, slot(stage, 0, 1), stage * 8 + 4, sibling)

    def step_z(stage):
        arrived(slot(stage, 0, 0))
        odd = lax.rem(stage, 2) == 1

        @pl.when(odd & (stage + 2 < NZ))
        def _():
            send(slot(stage, 0, 0), slot(stage + 2, 0, 0), stage * 8, z_up)

        @pl.when(jnp.logical_not(odd) & (stage + 2 < NZ))
        def _():
            send(slot(stage, 0, 0), slot(stage + 2, 0, 0), stage * 8, z_down)

        spread(stage)

    def step_y(stage):
        arrived(slot(stage, 1, 0))
        arrived(slot(stage, 3, 0))
        odd = lax.rem(stage, 2) == 1

        @pl.when(odd)
        def _():
            send(slot(stage, 3, 0), slot(stage, 2, 0), stage * 8 + 3, y_down)

        @pl.when(jnp.logical_not(odd))
        def _():
            send(slot(stage, 1, 0), slot(stage, 2, 0), stage * 8 + 3, y_up)

        send(slot(stage, 1, 0), slot(stage, 1, 1), stage * 8 + 5, sibling)
        send(slot(stage, 3, 0), slot(stage, 3, 1), stage * 8 + 7, sibling)

    def step_far(stage):
        arrived(slot(stage, 2, 0))
        send(slot(stage, 2, 0), slot(stage, 2, 1), stage * 8 + 6, sibling)

    def step_sibling(stage):
        for far in range(NY):
            arrived(slot(stage, far, 1))

    barrier = pltpu.get_barrier_semaphore()
    for neighbour in (z_up, z_down, y_up, y_down, sibling):
        pl.semaphore_signal(barrier, inc=1, device_id=neighbour, device_id_type=MESH)
    pl.semaphore_wait(barrier, 5)

    slots[0] = piece_ref[...]
    send(0, slot(1, 0, 0), 0, z_up)
    send(0, slot(2, 0, 0), 64, z_down)
    spread(0)

    def unit(keys, values, first):
        ones = jnp.ones((GRP, HD), jnp.bfloat16)
        for row in range(0, GRP, ROWS):
            for head in range(2):
                at = pl.ds(head * GRP + row, ROWS)
                last = row + ROWS if first else GRP
                scores = lax.dot_general(
                    q_ref[row : row + ROWS, head * HD : (head + 1) * HD],
                    slots[keys, 0:last, :],
                    (((1,), (1,)), ((), ())),
                    preferred_element_type=jnp.float32,
                )
                if first:
                    query_at = lax.broadcasted_iota(jnp.int32, (ROWS, last), 0) + row
                    key_at = lax.broadcasted_iota(jnp.int32, (ROWS, last), 1)
                    scores = jnp.where(key_at <= query_at, scores, NEG)
                block_top = jnp.max(scores, 1, keepdims=True) * EXP2_SCALE
                if first:
                    new_top = jnp.broadcast_to(block_top, (ROWS, HD))
                else:
                    old_top = top[at, :]
                    new_top = jnp.maximum(old_top, block_top)
                weights = jnp.exp2(scores * EXP2_SCALE - new_top[:, :1]).astype(jnp.bfloat16)
                gained = jnp.dot(
                    weights,
                    jnp.concatenate([slots[values, 0:last, :], ones[0:last]], 1),
                    preferred_element_type=jnp.float32,
                )
                top[at, :] = new_top
                if first:
                    accum[at, :] = gained
                else:
                    rescale = jnp.exp2(old_top - new_top)
                    accum[at, :] = accum[at, :] * jnp.concatenate([rescale, rescale], 1) + gained

    step_y(0)
    step_z(1)
    step_z(2)
    own_pair = 1 + 2 * (1 - y_lo)
    unit(slot(0, y_lo * own_pair, 0), slot(0, (1 - y_lo) * own_pair, 0), True)
    step_far(0)
    step_y(1)

    def body(index, carry):
        stage, part = lax.div(index, 4), lax.rem(index, 4)

        @pl.when(part == 0)
        def _():
            step_sibling(stage)

            @pl.when(stage + 3 < NZ)
            def _():
                step_z(stage + 3)

        @pl.when((part == 1) & (stage + 2 < NZ))
        def _():
            step_y(stage + 2)

        @pl.when((part == 2) & (stage + 1 < NZ))
        def _():
            step_far(stage + 1)

        hops = lax.div(stage + 1, 2)
        odd = lax.rem(stage, 2)
        from_z = odd * (z - hops) + (1 - odd) * (z + hops - NZ)
        live = ((stage == 0) & (part < place)) | ((stage > 0) & (from_z >= 0))

        @pl.when(live)
        def _():
            part_hi, part_core = lax.div(part, 2), lax.rem(part, 2)
            other = lax.rem(part_core + core, 2)
            unit(
                slot(stage, lax.rem(y - 2 * part_hi + NY, NY), other),
                slot(stage, lax.rem(y - 2 * part_hi - 1 + NY, NY), other),
                False,
            )

        return carry

    lax.fori_loop(0, 4 * NZ, body, 0)

    for row in range(0, GRP, ROWS):
        for head in range(2):
            at = pl.ds(head * GRP + row, ROWS)
            out_ref[row : row + ROWS, head * HD : (head + 1) * HD] = (
                accum[at, :HD] / accum[at, HD:]
            ).astype(jnp.bfloat16)

    sent(64)

    def finish(index, carry):
        stage, kind = lax.div(index, 8), lax.rem(index, 8)

        @pl.when((kind > 0) | (stage + 2 < NZ))
        def _():
            sent(index)

        return carry

    lax.fori_loop(0, 8 * NZ, finish, 0)


def attention(queries, piece):
    return pl.pallas_call(
        attention_kernel,
        out_shape=jax.ShapeDtypeStruct((GRP, 2 * HD), jnp.bfloat16),
        in_specs=[pl.BlockSpec(memory_space=pltpu.VMEM)] * 2,
        out_specs=pl.BlockSpec(memory_space=pltpu.VMEM),
        scratch_shapes=[
            pltpu.VMEM((8 * NZ, GRP, HD), jnp.bfloat16),
            pltpu.VMEM((2 * GRP, HD), jnp.float32),
            pltpu.VMEM((2 * GRP, 2 * HD), jnp.float32),
            pltpu.SemaphoreType.DMA((8 * NZ + 1,)),
            pltpu.SemaphoreType.DMA((8 * NZ,)),
        ],
        compiler_params=pltpu.CompilerParams(
            collective_id=0, has_side_effects=True, vmem_limit_bytes=44 * 1024 * 1024
        ),
        name="gather_attention",
    )(queries, piece)


def shards(
    frames,
    vis_gain,
    proj_weight,
    text_embed,
    text_lengths,
    norm_gain,
    q_weight,
    k_weight,
    v_weight,
    q_bias,
    k_bias,
    v_bias,
):
    uly_count = lax.axis_size("uly")
    slot_index = lax.axis_index("uly")
    group_index = lax.axis_index("blk")
    halo_frames = from_behind(frames[:2], "blk", -1)
    pooled = pool_frames(frames, halo_frames)
    normal_vis = layer_norm(pooled, vis_gain).astype(jnp.bfloat16)
    vis_rows = jnp.einsum(
        "fpv,vd->fpd",
        lax.all_gather(normal_vis, "uly", axis=1, tiled=True),
        proj_weight,
        preferred_element_type=jnp.float32,
    ).astype(jnp.bfloat16)
    vis_rows = vis_rows.reshape(-1, vis_rows.shape[-1])
    sequence = alternate(vis_rows, text_embed, text_lengths[0], PATCH)
    seq_float = sequence.astype(jnp.float32)
    row_sums = lax.psum(jnp.sum(seq_float * seq_float, 1), "uly")
    normalized_rows = (seq_float * lax.rsqrt(row_sums[:, None] / D + 1e-06) * norm_gain).astype(
        jnp.bfloat16
    )
    local_rows = q_weight.shape[0]
    q_cols = 2 * HD
    slot_q = q_weight.reshape(local_rows, uly_count, q_cols)
    slot_kv = jnp.stack(
        [k_weight.reshape(local_rows, KVH, HD), v_weight.reshape(local_rows, KVH, HD)], 2
    ).reshape(local_rows, uly_count, HD)
    slot_weight_matrix = jnp.concatenate([slot_q, slot_kv], 2)
    bias_kv = jnp.stack([k_bias.reshape(KVH, HD), v_bias.reshape(KVH, HD)], 1)
    slot_bias = lax.dynamic_index_in_dim(
        jnp.concatenate([q_bias.reshape(uly_count, q_cols), bias_kv.reshape(uly_count, HD)], 1),
        slot_index,
        0,
        keepdims=False,
    )
    seq_rows = normalized_rows.shape[0]
    partials = jnp.einsum(
        "wt,tai->awi", normalized_rows, slot_weight_matrix, preferred_element_type=jnp.float32
    ).astype(jnp.bfloat16)
    received = lax.all_to_all(partials, "uly", split_axis=0, concat_axis=0, tiled=True)
    projected = jnp.sum(received.astype(jnp.float32), 0) + slot_bias
    positions = group_index * seq_rows + jnp.arange(seq_rows, dtype=jnp.int32)
    inv_freq = jnp.power(
        jnp.float32(1000000.0), -jnp.arange(HD // 2, dtype=jnp.float32) * (2.0 / HD)
    )
    angles = positions.astype(jnp.float32)[:, None] * inv_freq[None]
    queries = rotate(projected[:, :q_cols].reshape(seq_rows, 2, HD), angles).reshape(
        seq_rows, q_cols
    )
    holds_keys = slot_index % 2 == 0
    rest = projected[:, q_cols:]
    piece = jnp.where(holds_keys, rotate(rest[:, None], angles)[:, 0], rest)
    return attention(queries.astype(jnp.bfloat16), piece.astype(jnp.bfloat16))


def solution(mesh):
    placed = (
        P("blk", "uly", None),
        P(),
        P(None, "uly"),
        P("blk", "uly"),
        P("blk", None),
        P("uly"),
        P("uly", None),
        P("uly", None),
        P("uly", None),
        P(),
        P(),
        P(),
    )
    return jax.shard_map(
        shards, mesh=mesh, in_specs=placed, out_specs=P("blk", "uly"), check_vma=False
    )
```

```python
import functools
import math

import jax
import jax.numpy as jnp
from jax import lax
from jax.experimental import pallas as pl
from jax.experimental.pallas import tpu as pltpu
from jax.sharding import PartitionSpec as P

PATCH = 64
D = 3584
HD = 128
GRP = 768
ROWS = 256
EXP2_SCALE = math.log2(math.e) / math.sqrt(HD)
NEG = -1e30
MESH = pl.DeviceIdType.MESH

NZ = 8
NY = 4


def attention_kernel(q_ref, piece_ref, out_ref, slots, top, accum, send_sem, recv_sem):
    blk = lax.axis_index("blk")
    uly = lax.axis_index("uly")
    z, place = lax.div(blk, 4), lax.rem(blk, 4)
    y_hi, core = lax.div(place, 2), lax.rem(place, 2)
    x, y_lo = lax.div(uly, 2), lax.rem(uly, 2)
    y = 2 * y_hi + y_lo

    def device(z_at, y_at, core_at):
        return (z_at * 4 + lax.div(y_at, 2) * 2 + core_at, x * 2 + lax.rem(y_at, 2))

    z_up = device(lax.rem(z + 1, NZ), y, core)
    z_down = device(lax.rem(z + NZ - 1, NZ), y, core)
    y_up = device(z, lax.rem(y + 1, NY), core)
    y_down = device(z, lax.rem(y + NY - 1, NY), core)
    sibling = device(z, y, 1 - core)

    def slot(stage, far, other):
        return stage * 8 + far * 2 + other

    def send(source, target, sem, to):
        pltpu.make_async_remote_copy(
            src_ref=slots.at[source],
            dst_ref=slots.at[target],
            send_sem=send_sem.at[sem],
            recv_sem=recv_sem.at[target],
            device_id=to,
            device_id_type=MESH,
        ).start()

    def arrived(target):
        pltpu.make_async_remote_copy(
            src_ref=slots.at[target],
            dst_ref=slots.at[target],
            send_sem=send_sem.at[target],
            recv_sem=recv_sem.at[target],
            device_id=sibling,
            device_id_type=MESH,
        ).wait_recv()

    def sent(sem):
        pltpu.make_async_remote_copy(
            src_ref=slots.at[0],
            dst_ref=slots.at[0],
            send_sem=send_sem.at[sem],
            recv_sem=recv_sem.at[0],
            device_id=sibling,
            device_id_type=MESH,
        ).wait_send()

    def spread(stage):
        mine = slot(stage, 0, 0)
        send(mine, slot(stage, 1, 0), stage * 8 + 1, y_up)
        send(mine, slot(stage, 3, 0), stage * 8 + 2, y_down)
        send(mine, slot(stage, 0, 1), stage * 8 + 4, sibling)

    def step_z(stage):
        arrived(slot(stage, 0, 0))
        odd = lax.rem(stage, 2) == 1

        @pl.when(odd & (stage + 2 < NZ))
        def _():
            send(slot(stage, 0, 0), slot(stage + 2, 0, 0), stage * 8, z_up)

        @pl.when(jnp.logical_not(odd) & (stage + 2 < NZ))
        def _():
            send(slot(stage, 0, 0), slot(stage + 2, 0, 0), stage * 8, z_down)

        spread(stage)

    def step_y(stage):
        arrived(slot(stage, 1, 0))
        arrived(slot(stage, 3, 0))
        odd = lax.rem(stage, 2) == 1

        @pl.when(odd)
        def _():
            send(slot(stage, 3, 0), slot(stage, 2, 0), stage * 8 + 3, y_down)

        @pl.when(jnp.logical_not(odd))
        def _():
            send(slot(stage, 1, 0), slot(stage, 2, 0), stage * 8 + 3, y_up)

        send(slot(stage, 1, 0), slot(stage, 1, 1), stage * 8 + 5, sibling)
        send(slot(stage, 3, 0), slot(stage, 3, 1), stage * 8 + 7, sibling)

    def step_far(stage):
        arrived(slot(stage, 2, 0))
        send(slot(stage, 2, 0), slot(stage, 2, 1), stage * 8 + 6, sibling)

    def step_sibling(stage):
        for far in range(NY):
            arrived(slot(stage, far, 1))

    barrier = pltpu.get_barrier_semaphore()
    for neighbour in (z_up, z_down, y_up, y_down, sibling):
        pl.semaphore_signal(barrier, inc=1, device_id=neighbour, device_id_type=MESH)
    pl.semaphore_wait(barrier, 5)

    slots[0] = piece_ref[...]
    send(0, slot(1, 0, 0), 0, z_up)
    send(0, slot(2, 0, 0), 64, z_down)
    spread(0)

    def unit(keys, values, first):
        ones = jnp.ones((GRP, HD), jnp.bfloat16)
        for row in range(0, GRP, ROWS):
            for head in range(2):
                at = pl.ds(head * GRP + row, ROWS)
                last = row + ROWS if first else GRP
                scores = lax.dot_general(
                    q_ref[row : row + ROWS, head * HD : (head + 1) * HD],
                    slots[keys, 0:last, :],
                    (((1,), (1,)), ((), ())),
                    preferred_element_type=jnp.float32,
                )
                if first:
                    query_at = lax.broadcasted_iota(jnp.int32, (ROWS, last), 0) + row
                    key_at = lax.broadcasted_iota(jnp.int32, (ROWS, last), 1)
                    scores = jnp.where(key_at <= query_at, scores, NEG)
                block_top = jnp.max(scores, 1, keepdims=True) * EXP2_SCALE
                if first:
                    new_top = jnp.broadcast_to(block_top, (ROWS, HD))
                else:
                    old_top = top[at, :]
                    new_top = jnp.maximum(old_top, block_top)
                weights = jnp.exp2(scores * EXP2_SCALE - new_top[:, :1]).astype(jnp.bfloat16)
                gained = jnp.dot(
                    weights,
                    jnp.concatenate([slots[values, 0:last, :], ones[0:last]], 1),
                    preferred_element_type=jnp.float32,
                )
                top[at, :] = new_top
                if first:
                    accum[at, :] = gained
                else:
                    rescale = jnp.exp2(old_top - new_top)
                    accum[at, :] = accum[at, :] * jnp.concatenate([rescale, rescale], 1) + gained

    step_y(0)
    step_z(1)
    step_z(2)
    own_pair = 1 + 2 * (1 - y_lo)
    unit(slot(0, y_lo * own_pair, 0), slot(0, (1 - y_lo) * own_pair, 0), True)
    step_far(0)
    step_y(1)

    def body(index, carry):
        stage, part = lax.div(index, 4), lax.rem(index, 4)

        @pl.when(part == 0)
        def _():
            step_sibling(stage)

            @pl.when(stage + 3 < NZ)
            def _():
                step_z(stage + 3)

        @pl.when((part == 1) & (stage + 2 < NZ))
        def _():
            step_y(stage + 2)

        @pl.when((part == 2) & (stage + 1 < NZ))
        def _():
            step_far(stage + 1)

        hops = lax.div(stage + 1, 2)
        odd = lax.rem(stage, 2)
        from_z = odd * (z - hops) + (1 - odd) * (z + hops - NZ)
        live = ((stage == 0) & (part < place)) | ((stage > 0) & (from_z >= 0))

        @pl.when(live)
        def _():
            part_hi, part_core = lax.div(part, 2), lax.rem(part, 2)
            other = lax.rem(part_core + core, 2)
            unit(
                slot(stage, lax.rem(y - 2 * part_hi + NY, NY), other),
                slot(stage, lax.rem(y - 2 * part_hi - 1 + NY, NY), other),
                False,
            )

        return carry

    lax.fori_loop(0, 4 * NZ, body, 0)

    for row in range(0, GRP, ROWS):
        for head in range(2):
            at = pl.ds(head * GRP + row, ROWS)
            out_ref[row : row + ROWS, head * HD : (head + 1) * HD] = (
                accum[at, :HD] / accum[at, HD:]
            ).astype(jnp.bfloat16)

    sent(64)

    def finish(index, carry):
        stage, kind = lax.div(index, 8), lax.rem(index, 8)

        @pl.when((kind > 0) | (stage + 2 < NZ))
        def _():
            sent(index)

        return carry

    lax.fori_loop(0, 8 * NZ, finish, 0)


def attention(queries, piece):
    return pl.pallas_call(
        attention_kernel,
        out_shape=jax.ShapeDtypeStruct((GRP, 2 * HD), jnp.bfloat16),
        in_specs=[pl.BlockSpec(memory_space=pltpu.VMEM)] * 2,
        out_specs=pl.BlockSpec(memory_space=pltpu.VMEM),
        scratch_shapes=[
            pltpu.VMEM((8 * NZ, GRP, HD), jnp.bfloat16),
            pltpu.VMEM((2 * GRP, HD), jnp.float32),
            pltpu.VMEM((2 * GRP, 2 * HD), jnp.float32),
            pltpu.SemaphoreType.DMA((8 * NZ + 1,)),
            pltpu.SemaphoreType.DMA((8 * NZ,)),
        ],
        compiler_params=pltpu.CompilerParams(
            collective_id=0, has_side_effects=True, vmem_limit_bytes=44 * 1024 * 1024
        ),
        name="gather_attention",
    )(queries, piece)


TEXT_GRP = 512
CHUNK = 128
CHUNKS = GRP // CHUNK
COLS = 3 * HD
V = 1152


def project_kernel(
    frames_ref,
    vis_gain_ref,
    proj_ref,
    text_ref,
    lengths_ref,
    gain_ref,
    wq_ref,
    wk_ref,
    wv_ref,
    bq_ref,
    bk_ref,
    bv_ref,
    freq_ref,
    q_ref,
    piece_ref,
    halo,
    gathered,
    rows,
    vis,
    text_sums,
    vis_sums,
    far_out,
    far_in,
    near_out,
    near_in,
    pair_out,
    pair_in,
    kept,
    cosine,
    sine,
    done,
    send_sem,
    recv_sem,
):
    blk = lax.axis_index("blk")
    uly = lax.axis_index("uly")
    n_blk = lax.axis_size("blk")
    x, y_lo = lax.div(uly, 2), lax.rem(uly, 2)
    x_up, x_down, x_far = lax.rem(x + 1, 4), lax.rem(x + 3, 4), lax.rem(x + 2, 4)
    up, down, pair = (blk, x_up * 2 + y_lo), (blk, x_down * 2 + y_lo), (blk, x * 2 + 1 - y_lo)
    peers = [None] + [(blk, lax.rem(uly + step, 8)) for step in range(1, 8)]
    earlier = (lax.rem(blk + n_blk - 1, n_blk), uly)
    later = (lax.rem(blk + 1, n_blk), uly)
    text_at, vis_at, gather_at, far_at, near_at, pair_at = 0, 8, 16, 24, 36, 48

    def copy(source, target, sem, to):
        return pltpu.make_async_remote_copy(
            src_ref=source,
            dst_ref=target,
            send_sem=send_sem.at[sem],
            recv_sem=recv_sem.at[sem],
            device_id=to,
            device_id_type=MESH,
        )

    barrier = pltpu.get_barrier_semaphore()
    for other in peers[1:] + [earlier, later]:
        pl.semaphore_signal(barrier, inc=1, device_id=other, device_id_type=MESH)
    pl.semaphore_wait(barrier, 9)

    halo_copy = copy(frames_ref.at[0:2], halo, 0, earlier)
    halo_copy.start()
    copies = [halo_copy]

    def share_sums(values, sums, base):
        squares = jnp.sum(values * values, 1, keepdims=True)
        sums[0] = jnp.transpose(jnp.broadcast_to(squares, (values.shape[0], 128)))[0:8]
        for step in range(1, 8):
            sums_copy = copy(sums.at[0], sums.at[step], base + step, peers[step])
            sums_copy.start()
            copies.append(sums_copy)

    def scales(sums, base):
        for step in range(1, 8):
            copy(sums.at[step], sums.at[step], base + step, peers[step]).wait_recv()
        total = sums[0]
        for step in range(1, 8):
            total = total + sums[step]
        inverse = lax.rsqrt(total[0:1] / D + 1e-06)
        return jnp.transpose(jnp.broadcast_to(inverse, (128, inverse.shape[1])))[:, 0:1]

    share_sums(text_ref[...].astype(jnp.float32), text_sums, text_at)

    halo_copy.wait_recv()
    tail = jnp.where(blk < n_blk - 1, halo[...].astype(jnp.float32), 0.0)
    frames = frames_ref[...].astype(jnp.float32)
    pairs = [frames[2 * i] + frames[2 * i + 1] for i in range(4)] + [tail[0] + tail[1]]
    for i in range(4):
        pooled = (pairs[i] + pairs[i + 1]) * 0.25
        centred = pooled - jnp.mean(pooled, -1, keepdims=True)
        variance = jnp.mean(centred * centred, -1, keepdims=True)
        normal = centred * lax.rsqrt(variance + 1e-06) * vis_gain_ref[...]
        kept[0, 8 * i : 8 * i + 8, :] = normal[:, 0:COLS]
        kept[1, 8 * i : 8 * i + 8, :] = normal[:, COLS : 2 * COLS]
        kept[2, 8 * i : 8 * i + 8, :] = normal[:, 2 * COLS :]
    for i in range(3):
        gathered[uly, :, COLS * i : COLS * i + COLS] = kept[i, 0:32, :].astype(jnp.bfloat16)
    for step in range(1, 8):
        gather_copy = copy(gathered.at[uly], gathered.at[uly], gather_at + step, peers[step])
        gather_copy.start()
        copies.append(gather_copy)

    def normalize(values, scale, start):
        rows[start : start + values.shape[0], :] = (values * scale * gain_ref[...]).astype(
            jnp.bfloat16
        )

    normalize(text_ref[...].astype(jnp.float32), scales(text_sums, text_at), 0)

    def partial(chunk, x_at, first, last):
        left = rows[chunk * CHUNK + first : chunk * CHUNK + last, :]
        parts = []
        for half, other_ref in ((0, wk_ref), (1, wv_ref)):
            q_at = pl.multiple_of(x_at * 4 * HD + half * 2 * HD, 2 * HD)
            kv_at = pl.multiple_of(x_at * HD, HD)
            for weight in (wq_ref[:, pl.ds(q_at, 2 * HD)], other_ref[:, pl.ds(kv_at, HD)]):
                parts.append(jnp.dot(left, weight, preferred_element_type=jnp.float32))
        return jnp.concatenate(parts, 1)

    half = CHUNK // 2

    def far_copies(chunk):
        return (
            copy(far_out.at[chunk, 0:half], far_in.at[chunk, 0:half], far_at + 2 * chunk, up),
            copy(far_out.at[chunk, half:], far_in.at[chunk, half:], far_at + 2 * chunk + 1, down),
        )

    def near_copies(chunk):
        return (
            copy(near_out.at[chunk, 0], near_in.at[chunk, 0], near_at + 2 * chunk, up),
            copy(near_out.at[chunk, 1], near_in.at[chunk, 1], near_at + 2 * chunk + 1, down),
        )

    def pair_copy(chunk):
        return copy(pair_out.at[chunk], pair_in.at[chunk], pair_at + chunk, pair)

    def send_far(chunk):
        far_out[chunk] = partial(chunk, x_far, 0, CHUNK).astype(jnp.bfloat16)
        for each in far_copies(chunk):
            each.start()
            copies.append(each)

    def send_near(chunk):
        for each in far_copies(chunk):
            each.wait_recv()
        for way, x_at, relayed in ((0, x_up, 0), (1, x_down, 1)):
            own = partial(chunk, x_at, 0, CHUNK)
            at = slice(relayed * half, relayed * half + half)
            rest = slice((1 - relayed) * half, (1 - relayed) * half + half)
            near_out[chunk, way, at, :] = (
                own[at] + far_in[chunk, at, :].astype(jnp.float32)
            ).astype(jnp.bfloat16)
            near_out[chunk, way, rest, :] = own[rest].astype(jnp.bfloat16)
        for each in near_copies(chunk):
            each.start()
            copies.append(each)

    def send_pair(chunk):
        for each in near_copies(chunk):
            each.wait_recv()
        total = (
            partial(chunk, x, 0, CHUNK)
            + near_in[chunk, 0].astype(jnp.float32)
            + near_in[chunk, 1].astype(jnp.float32)
        )
        low, high = total[:, :COLS], total[:, COLS:]
        mine = jnp.where(y_lo == 0, low, high)
        pair_out[chunk] = jnp.where(y_lo == 0, high, low).astype(jnp.bfloat16)
        kept[chunk] = mine
        each = pair_copy(chunk)
        each.start()
        copies.append(each)

    def run_ends():
        ends = [lengths_ref[0, 0]]
        for run in range(1, 4):
            ends.append(ends[-1] + lengths_ref[0, run])
        return ends

    def text_places(index):
        place = index
        for end in run_ends():
            place = place + jnp.where(index >= end, PATCH, 0)
        return place

    def vis_places(index):
        frame = (index >> 3) & 3
        place = (index >> 5) * 8 + (index & 7)
        for number, end in enumerate(run_ends()):
            place = place + jnp.where(frame == number, end + PATCH * number, 0)
        return place

    def angles(start, count, places):
        index = lax.broadcasted_iota(jnp.int32, (count, HD), 0)
        angle = (blk * GRP + places(index)).astype(jnp.float32) * freq_ref[...]
        lane = lax.broadcasted_iota(jnp.int32, (count, HD), 1)
        cosine[start : start + count, :] = jnp.cos(angle)
        turned = jnp.sin(angle)
        sine[start : start + count, :] = jnp.where(lane < HD // 2, -turned, turned)

    def finish(chunk):
        pair_copy(chunk).wait_recv()
        at = slice(chunk * CHUNK, chunk * CHUNK + CHUNK)
        total = kept[chunk] + pair_in[chunk].astype(jnp.float32)
        kv_at = pl.multiple_of(x * HD, HD)
        kv_bias = jnp.where(y_lo == 0, bk_ref[:, pl.ds(kv_at, HD)], bv_ref[:, pl.ds(kv_at, HD)])
        q_bias = bq_ref[:, pl.ds(pl.multiple_of(uly * 2 * HD, 2 * HD), 2 * HD)]
        for part, bias in enumerate((q_bias[:, :HD], q_bias[:, HD:], kv_bias)):
            plain = total[:, part * HD : part * HD + HD] + bias
            turned = plain * cosine[at, :] + pltpu.roll(plain, HD // 2, 1) * sine[at, :]
            if part == 2:
                turned = jnp.where(y_lo == 0, turned, plain)
            done[at, part * HD : part * HD + HD] = turned.astype(jnp.bfloat16)

    for chunk in range(4):
        send_far(chunk)
    for step in range(1, 8):
        source = lax.rem(uly + 8 - step, 8)
        copy(gathered.at[source], gathered.at[source], gather_at + step, peers[step]).wait_recv()
    vis[...] = jnp.dot(
        gathered[...].reshape(GRP - TEXT_GRP, V), proj_ref[...], preferred_element_type=jnp.float32
    ).astype(jnp.bfloat16)
    share_sums(vis[...].astype(jnp.float32), vis_sums, vis_at)
    send_near(0)
    send_near(1)
    normalize(vis[...].astype(jnp.float32), scales(vis_sums, vis_at), TEXT_GRP)
    send_far(4)
    send_far(5)
    send_near(2)
    send_near(3)
    angles(0, TEXT_GRP, text_places)
    angles(TEXT_GRP, GRP - TEXT_GRP, vis_places)
    send_near(4)
    send_near(5)
    for chunk in range(4):
        send_pair(chunk)
    for chunk in range(3):
        finish(chunk)
    send_pair(4)
    finish(3)
    send_pair(5)
    finish(4)
    finish(5)

    index = lax.broadcasted_iota(jnp.int32, (CHUNK, TEXT_GRP), 1)
    vis_index = lax.broadcasted_iota(jnp.int32, (CHUNK, GRP - TEXT_GRP), 1)
    places = jnp.concatenate([text_places(index), vis_places(vis_index)], 1)
    wanted = lax.broadcasted_iota(jnp.int32, (CHUNK, GRP), 0)
    for chunk in range(CHUNKS):
        at = slice(chunk * CHUNK, chunk * CHUNK + CHUNK)
        chosen = jnp.where(places == wanted + chunk * CHUNK, 1.0, 0.0).astype(jnp.bfloat16)
        ordered = jnp.dot(chosen, done[...], preferred_element_type=jnp.float32)
        q_ref[at, :] = ordered[:, : 2 * HD].astype(jnp.bfloat16)
        piece_ref[at, :] = ordered[:, 2 * HD :].astype(jnp.bfloat16)

    for each in copies:
        each.wait_send()


def project(*operands):
    vmem = pl.BlockSpec(memory_space=pltpu.VMEM)
    in_specs = [vmem] * 4 + [pl.BlockSpec(memory_space=pltpu.SMEM)] + [vmem] * 8
    bf16, f32 = jnp.bfloat16, jnp.float32
    features = operands[3].shape[1]
    return pl.pallas_call(
        project_kernel,
        out_shape=(
            jax.ShapeDtypeStruct((GRP, 2 * HD), bf16),
            jax.ShapeDtypeStruct((GRP, HD), bf16),
        ),
        in_specs=in_specs,
        out_specs=(vmem, vmem),
        scratch_shapes=[
            pltpu.VMEM((2, 8, V), bf16),
            pltpu.VMEM((8, 32, V), bf16),
            pltpu.VMEM((GRP, features), bf16),
            pltpu.VMEM((GRP - TEXT_GRP, features), bf16),
            pltpu.VMEM((8, 8, TEXT_GRP), f32),
            pltpu.VMEM((8, 8, GRP - TEXT_GRP), f32),
            pltpu.VMEM((CHUNKS, CHUNK, 2 * COLS), bf16),
            pltpu.VMEM((CHUNKS, CHUNK, 2 * COLS), bf16),
            pltpu.VMEM((CHUNKS, 2, CHUNK, 2 * COLS), bf16),
            pltpu.VMEM((CHUNKS, 2, CHUNK, 2 * COLS), bf16),
            pltpu.VMEM((CHUNKS, CHUNK, COLS), bf16),
            pltpu.VMEM((CHUNKS, CHUNK, COLS), bf16),
            pltpu.VMEM((CHUNKS, CHUNK, COLS), f32),
            pltpu.VMEM((GRP, HD), f32),
            pltpu.VMEM((GRP, HD), f32),
            pltpu.VMEM((GRP, COLS), bf16),
            pltpu.SemaphoreType.DMA((54,)),
            pltpu.SemaphoreType.DMA((54,)),
        ],
        compiler_params=pltpu.CompilerParams(
            collective_id=1, has_side_effects=True, vmem_limit_bytes=44 * 1024 * 1024
        ),
        name="project",
    )(*operands)


def shards(
    frames,
    vis_gain,
    proj_weight,
    text_embed,
    text_lengths,
    norm_gain,
    q_weight,
    k_weight,
    v_weight,
    q_bias,
    k_bias,
    v_bias,
):
    inv_freq = jnp.power(
        jnp.float32(1000000.0), -jnp.arange(HD // 2, dtype=jnp.float32) * (2.0 / HD)
    )
    queries, piece = project(
        frames,
        vis_gain[None],
        proj_weight,
        text_embed,
        text_lengths,
        norm_gain[None],
        q_weight,
        k_weight,
        v_weight,
        q_bias[None],
        k_bias[None],
        v_bias[None],
        jnp.concatenate([inv_freq, inv_freq])[None],
    )
    return attention(queries, piece)


def solution(mesh):
    placed = (
        P("blk", "uly", None),
        P(),
        P(None, "uly"),
        P("blk", "uly"),
        P("blk", None),
        P("uly"),
        P("uly", None),
        P("uly", None),
        P("uly", None),
        P(),
        P(),
        P(),
    )
    return jax.shard_map(
        shards, mesh=mesh, in_specs=placed, out_specs=P("blk", "uly"), check_vma=False
    )
```

```python
import math

import jax
import jax.numpy as jnp
import numpy as np
from jax import lax
from jax.experimental import pallas as pl
from jax.experimental.pallas import tpu as pltpu
from jax.sharding import PartitionSpec as P

PATCH = 64
D = 3584
V = 1152
HD = 128
GRP = 768
TEXT_GRP = 512
VIS_GRP = 256
CHUNK = 128
CHUNKS = GRP // CHUNK
ROWS = 256
EXP2_SCALE = math.log2(math.e) / math.sqrt(HD)
NEG = -1e30
MESH = pl.DeviceIdType.MESH

NZ = 8
NY = 4

KV, Q = 0, 1
WIDTH = (2 * HD, 4 * HD)

AT_HALO, AT_TEXT, AT_VIS, AT_GATHER = 0, 0, 8, 16
AT_FAR, AT_NEAR, AT_PAIR = (24, 36), (48, 60), (72, 78)
AT_SLOTS = 84


def kernel(
    frames_hbm,
    vis_gain_hbm,
    proj_hbm,
    text_hbm,
    lengths_hbm,
    gain_hbm,
    wq_hbm,
    wk_hbm,
    wv_hbm,
    bq_hbm,
    bk_hbm,
    bv_hbm,
    freq_hbm,
    out_ref,
    frames_ref,
    vis_gain_ref,
    proj_ref,
    text_ref,
    lengths_ref,
    gain_ref,
    wq_ref,
    wk_ref,
    wv_ref,
    bq_ref,
    bk_ref,
    bv_ref,
    freq_ref,
    halo,
    normal_rows,
    gathered,
    rows,
    vis,
    text_sums,
    vis_sums,
    far_out_kv,
    far_in_kv,
    near_out_kv,
    near_in_kv,
    pair_out_kv,
    pair_in_kv,
    kept_kv,
    far_out_q,
    far_in_q,
    near_out_q,
    near_in_q,
    pair_out_q,
    pair_in_q,
    kept_q,
    cosine,
    sine,
    done_kv,
    done_q,
    queries,
    slots,
    top,
    accum,
    load_sem,
    send_sem,
    recv_sem,
):
    blk = lax.axis_index("blk")
    uly = lax.axis_index("uly")
    n_blk = lax.axis_size("blk")
    z, place = lax.div(blk, 4), lax.rem(blk, 4)
    y_hi, core = lax.div(place, 2), lax.rem(place, 2)
    x, y_lo = lax.div(uly, 2), lax.rem(uly, 2)
    y = 2 * y_hi + y_lo

    loads = [
        pltpu.make_async_copy(source, target, load_sem.at[number])
        for number, (source, target) in enumerate(
            (
                (frames_hbm, frames_ref),
                (text_hbm, text_ref),
                (vis_gain_hbm, vis_gain_ref),
                (gain_hbm, gain_ref),
                (wk_hbm, wk_ref),
                (wv_hbm, wv_ref),
                (proj_hbm, proj_ref),
                (lengths_hbm, lengths_ref),
                (freq_hbm, freq_ref),
                (bk_hbm, bk_ref),
                (bv_hbm, bv_ref),
                (bq_hbm, bq_ref),
                (wq_hbm, wq_ref),
            )
        )
    ]
    for load in loads:
        load.start()

    def device(z_at, y_at, core_at):
        return (z_at * 4 + lax.div(y_at, 2) * 2 + core_at, x * 2 + lax.rem(y_at, 2))

    z_up = device(lax.rem(z + 1, NZ), y, core)
    z_down = device(lax.rem(z + NZ - 1, NZ), y, core)
    y_up = device(z, lax.rem(y + 1, NY), core)
    y_down = device(z, lax.rem(y + NY - 1, NY), core)
    sibling = device(z, y, 1 - core)
    x_up, x_down, x_far = lax.rem(x + 1, 4), lax.rem(x + 3, 4), lax.rem(x + 2, 4)
    up, down, pair = (blk, x_up * 2 + y_lo), (blk, x_down * 2 + y_lo), (blk, x * 2 + 1 - y_lo)
    peers = [None] + [(blk, lax.rem(uly + step, 8)) for step in range(1, 8)]
    earlier = (lax.rem(blk + n_blk - 1, n_blk), uly)
    later = (lax.rem(blk + 1, n_blk), uly)

    barrier = pltpu.get_barrier_semaphore()
    others = peers[1:] + [earlier, later, z_up, z_down, y_up, y_down, sibling]
    for other in others:
        pl.semaphore_signal(barrier, inc=1, device_id=other, device_id_type=MESH)
    pl.semaphore_wait(barrier, len(others))

    copies = []

    def copy(source, target, sem, to):
        return pltpu.make_async_remote_copy(
            src_ref=source,
            dst_ref=target,
            send_sem=send_sem.at[sem],
            recv_sem=recv_sem.at[sem],
            device_id=to,
            device_id_type=MESH,
        )

    def start(each):
        each.start()
        copies.append(each)

    loads[0].wait()
    halo_copy = copy(frames_ref.at[0:2], halo, AT_HALO, earlier)
    start(halo_copy)

    def send_sums(sums, base):
        for step in range(1, 8):
            start(copy(sums.at[0], sums.at[step], base + step, peers[step]))

    def scales(sums, base):
        for step in range(1, 8):
            copy(sums.at[step], sums.at[step], base + step, peers[step]).wait_recv()
        total = sums[0]
        for step in range(1, 8):
            total = total + sums[step]
        return lax.rsqrt(total[0:1] / D + 1e-06)

    loads[1].wait()
    text = text_ref[...].astype(jnp.float32)
    text_sums[0] = jnp.broadcast_to(jnp.sum(text * text, 0, keepdims=True), (8, TEXT_GRP))
    send_sums(text_sums, AT_TEXT)

    for load in loads[2:6]:
        load.wait()
    halo_copy.wait_recv()
    tail = jnp.where(blk < n_blk - 1, halo[...].astype(jnp.float32), 0.0)
    frames = frames_ref[...].astype(jnp.float32)
    pairs = [frames[2 * i] + frames[2 * i + 1] for i in range(4)] + [tail[0] + tail[1]]
    for i in range(4):
        pooled = (pairs[i] + pairs[i + 1]) * 0.25
        centred = pooled - jnp.mean(pooled, -1, keepdims=True)
        variance = jnp.mean(centred * centred, -1, keepdims=True)
        normal_rows[8 * i : 8 * i + 8, :] = (
            centred * lax.rsqrt(variance + 1e-06) * vis_gain_ref[...]
        )
    gathered[uly] = normal_rows[...].astype(jnp.bfloat16)
    for step in range(1, 8):
        start(copy(gathered.at[uly], gathered.at[uly], AT_GATHER + step, peers[step]))

    scaled_text = jnp.transpose(text_ref[...].astype(jnp.float32) * scales(text_sums, AT_TEXT))
    rows[0:TEXT_GRP, :] = (scaled_text * gain_ref[...]).astype(jnp.bfloat16)

    far_out, far_in = (far_out_kv, far_out_q), (far_in_kv, far_in_q)
    near_out, near_in = (near_out_kv, near_out_q), (near_in_kv, near_in_q)
    pair_out, pair_in = (pair_out_kv, pair_out_q), (pair_in_kv, pair_in_q)
    kept, done = (kept_kv, kept_q), (done_kv, done_q)
    half = CHUNK // 2

    def partial(kind, chunk, x_at):
        left = rows[chunk * CHUNK : (chunk + 1) * CHUNK, :]
        if kind == Q:
            weight = wq_ref[:, pl.ds(pl.multiple_of(x_at * 4 * HD, 4 * HD), 4 * HD)]
            return jnp.dot(left, weight, preferred_element_type=jnp.float32)
        at = pl.ds(pl.multiple_of(x_at * HD, HD), HD)
        return jnp.concatenate(
            [
                jnp.dot(left, weight[:, at], preferred_element_type=jnp.float32)
                for weight in (wk_ref, wv_ref)
            ],
            1,
        )

    def far_copies(kind, chunk):
        out, into, base = far_out[kind].at[chunk], far_in[kind].at[chunk], AT_FAR[kind] + 2 * chunk
        return (
            copy(out.at[0:half], into.at[0:half], base, up),
            copy(out.at[half:CHUNK], into.at[half:CHUNK], base + 1, down),
        )

    def near_copies(kind, chunk):
        out, into = near_out[kind].at[chunk], near_in[kind].at[chunk]
        base = AT_NEAR[kind] + 2 * chunk
        return (
            copy(out.at[0], into.at[0], base, up),
            copy(out.at[1], into.at[1], base + 1, down),
        )

    def pair_copy(kind, chunk):
        return copy(
            pair_out[kind].at[chunk], pair_in[kind].at[chunk], AT_PAIR[kind] + chunk, pair
        )

    def send_far(kind, chunk):
        far_out[kind][chunk] = partial(kind, chunk, x_far).astype(jnp.bfloat16)
        for each in far_copies(kind, chunk):
            start(each)

    def send_near(kind, chunk):
        for each in far_copies(kind, chunk):
            each.wait_recv()
        for way, x_at in ((0, x_up), (1, x_down)):
            own = partial(kind, chunk, x_at)
            relayed = slice(way * half, way * half + half)
            rest = slice((1 - way) * half, (1 - way) * half + half)
            near_out[kind][chunk, way, relayed, :] = (
                own[relayed] + far_in[kind][chunk, relayed, :].astype(jnp.float32)
            ).astype(jnp.bfloat16)
            near_out[kind][chunk, way, rest, :] = own[rest].astype(jnp.bfloat16)
        for each in near_copies(kind, chunk):
            start(each)

    def send_pair(kind, chunk):
        for each in near_copies(kind, chunk):
            each.wait_recv()
        total = (
            partial(kind, chunk, x)
            + near_in[kind][chunk, 0].astype(jnp.float32)
            + near_in[kind][chunk, 1].astype(jnp.float32)
        )
        middle = WIDTH[kind] // 2
        low, high = total[:, :middle], total[:, middle:]
        kept[kind][chunk] = jnp.where(y_lo == 0, low, high)
        pair_out[kind][chunk] = jnp.where(y_lo == 0, high, low).astype(jnp.bfloat16)
        start(pair_copy(kind, chunk))

    def finish(kind, chunk):
        pair_copy(kind, chunk).wait_recv()
        at = slice(chunk * CHUNK, chunk * CHUNK + CHUNK)
        total = kept[kind][chunk] + pair_in[kind][chunk].astype(jnp.float32)
        if kind == KV:
            bias_at = pl.ds(pl.multiple_of(x * HD, HD), HD)
            total = total + jnp.where(y_lo == 0, bk_ref[:, bias_at], bv_ref[:, bias_at])
        else:
            total = total + bq_ref[:, pl.ds(pl.multiple_of(uly * 2 * HD, 2 * HD), 2 * HD)]
        for head in range(WIDTH[kind] // (2 * HD)):
            columns = slice(head * HD, head * HD + HD)
            plain = total[:, columns]
            turned = plain * cosine[at, :] + pltpu.roll(plain, HD // 2, 1) * sine[at, :]
            if kind == KV:
                turned = jnp.where(y_lo == 0, turned, plain)
            done[kind][at, columns] = turned.astype(jnp.bfloat16)

    def run_ends():
        ends = [lengths_ref[0, 0]]
        for run in range(1, 4):
            ends.append(ends[-1] + lengths_ref[0, run])
        return ends

    def text_places(index):
        place_of = index
        for end in run_ends():
            place_of = place_of + jnp.where(index >= end, PATCH, 0)
        return place_of

    def vis_places(index):
        frame = (index >> 3) & 3
        place_of = (index >> 5) * 8 + (index & 7)
        for number, end in enumerate(run_ends()):
            place_of = place_of + jnp.where(frame == number, end + PATCH * number, 0)
        return place_of

    def angles(first, count, places):
        index = lax.broadcasted_iota(jnp.int32, (count, HD), 0)
        angle = (blk * GRP + places(index)).astype(jnp.float32) * freq_ref[...]
        lane = lax.broadcasted_iota(jnp.int32, (count, HD), 1)
        cosine[first : first + count, :] = jnp.cos(angle)
        turned = jnp.sin(angle)
        sine[first : first + count, :] = jnp.where(lane < HD // 2, -turned, turned)

    def ordered(kind, write):
        index = lax.broadcasted_iota(jnp.int32, (CHUNK, TEXT_GRP), 1)
        vis_index = lax.broadcasted_iota(jnp.int32, (CHUNK, VIS_GRP), 1)
        places = jnp.concatenate([text_places(index), vis_places(vis_index)], 1)
        wanted = lax.broadcasted_iota(jnp.int32, (CHUNK, GRP), 0)
        for chunk in range(CHUNKS):
            chosen = jnp.where(places == wanted + chunk * CHUNK, 1.0, 0.0).astype(jnp.bfloat16)
            result = jnp.dot(chosen, done[kind][...], preferred_element_type=jnp.float32)
            write(slice(chunk * CHUNK, chunk * CHUNK + CHUNK), result.astype(jnp.bfloat16))

    def slot(stage, far, other):
        return stage * 8 + far * 2 + other

    def slot_copy(source, target, sem, to):
        return pltpu.make_async_remote_copy(
            src_ref=slots.at[source],
            dst_ref=slots.at[target],
            send_sem=send_sem.at[AT_SLOTS + sem],
            recv_sem=recv_sem.at[AT_SLOTS + target],
            device_id=to,
            device_id_type=MESH,
        )

    def send(source, target, sem, to):
        slot_copy(source, target, sem, to).start()

    def arrived(target):
        slot_copy(target, target, target, sibling).wait_recv()

    def spread(stage):
        mine = slot(stage, 0, 0)
        send(mine, slot(stage, 1, 0), stage * 8 + 1, y_up)
        send(mine, slot(stage, 3, 0), stage * 8 + 2, y_down)
        send(mine, slot(stage, 0, 1), stage * 8 + 4, sibling)

    def step_z(stage):
        arrived(slot(stage, 0, 0))
        odd = lax.rem(stage, 2) == 1

        @pl.when(odd & (stage + 2 < NZ))
        def _():
            send(slot(stage, 0, 0), slot(stage + 2, 0, 0), stage * 8, z_up)

        @pl.when(jnp.logical_not(odd) & (stage + 2 < NZ))
        def _():
            send(slot(stage, 0, 0), slot(stage + 2, 0, 0), stage * 8, z_down)

        spread(stage)

    def step_y(stage):
        arrived(slot(stage, 1, 0))
        arrived(slot(stage, 3, 0))
        odd = lax.rem(stage, 2) == 1

        @pl.when(odd)
        def _():
            send(slot(stage, 3, 0), slot(stage, 2, 0), stage * 8 + 3, y_down)

        @pl.when(jnp.logical_not(odd))
        def _():
            send(slot(stage, 1, 0), slot(stage, 2, 0), stage * 8 + 3, y_up)

        send(slot(stage, 1, 0), slot(stage, 1, 1), stage * 8 + 5, sibling)
        send(slot(stage, 3, 0), slot(stage, 3, 1), stage * 8 + 7, sibling)

    def step_far(stage):
        arrived(slot(stage, 2, 0))
        send(slot(stage, 2, 0), slot(stage, 2, 1), stage * 8 + 6, sibling)

    def step_sibling(stage):
        for far in range(NY):
            arrived(slot(stage, far, 1))

    def scores_of(keys, count, row, head, last):
        block = slots[pl.ds(keys, count), 0:last, :].reshape(count * last, HD)
        return lax.dot_general(
            queries[row : row + ROWS, head * HD : (head + 1) * HD],
            block,
            (((1,), (1,)), ((), ())),
            preferred_element_type=jnp.float32,
        )

    def absorb(values, count, row, head, last, scores, first):
        at = pl.ds(head * GRP + row, ROWS)
        if first:
            query_at = lax.broadcasted_iota(jnp.int32, (ROWS, last), 0) + row
            key_at = lax.broadcasted_iota(jnp.int32, (ROWS, last), 1)
            scores = jnp.where(key_at <= query_at, scores, NEG)
        block_top = jnp.max(scores, 1, keepdims=True) * EXP2_SCALE
        if first:
            new_top = jnp.broadcast_to(block_top, (ROWS, HD))
        else:
            old_top = top[at, :]
            new_top = jnp.maximum(old_top, block_top)
        weights = jnp.exp2(scores * EXP2_SCALE - new_top[:, :1]).astype(jnp.bfloat16)
        block = slots[pl.ds(values, count), 0:last, :].reshape(count * last, HD)
        gained = jnp.dot(
            weights,
            jnp.concatenate([block, jnp.ones(block.shape, jnp.bfloat16)], 1),
            preferred_element_type=jnp.float32,
        )
        top[at, :] = new_top
        if first:
            accum[at, :] = gained
        else:
            rescale = jnp.exp2(old_top - new_top)
            accum[at, :] = accum[at, :] * jnp.concatenate([rescale, rescale], 1) + gained

    def unit(keys, values, count, first):
        waiting = None
        for row in range(0, GRP, ROWS):
            for head in range(2):
                last = row + ROWS if first else GRP
                scores = scores_of(keys, count, row, head, last)
                if waiting is not None:
                    absorb(values, count, *waiting, first)
                waiting = (row, head, last, scores)
        absorb(values, count, *waiting, first)

    for chunk in range(4):
        send_far(KV, chunk)
    loads[6].wait()
    for step in range(1, 8):
        source = lax.rem(uly + 8 - step, 8)
        copy(gathered.at[source], gathered.at[source], AT_GATHER + step, peers[step]).wait_recv()
    vis[...] = lax.dot_general(
        gathered[...].reshape(VIS_GRP, V),
        proj_ref[...],
        (((1,), (1,)), ((), ())),
        preferred_element_type=jnp.float32,
    ).astype(jnp.bfloat16)
    vis_float = vis[...].astype(jnp.float32)
    squares = jnp.sum(vis_float * vis_float, 1, keepdims=True)
    vis_sums[0] = jnp.transpose(jnp.broadcast_to(squares, (VIS_GRP, 128)))[0:8]
    send_sums(vis_sums, AT_VIS)
    for chunk in range(4):
        send_near(KV, chunk)
    inverse = jnp.transpose(jnp.broadcast_to(scales(vis_sums, AT_VIS), (128, VIS_GRP)))[:, 0:1]
    rows[TEXT_GRP:GRP, :] = (vis[...].astype(jnp.float32) * inverse * gain_ref[...]).astype(
        jnp.bfloat16
    )
    send_far(KV, 4)
    send_far(KV, 5)
    for load in loads[7:]:
        load.wait()
    for chunk in range(4):
        send_far(Q, chunk)
    angles(0, TEXT_GRP, text_places)
    send_near(KV, 4)
    send_near(KV, 5)
    for chunk in range(4):
        send_pair(KV, chunk)
    angles(TEXT_GRP, VIS_GRP, vis_places)
    for chunk in range(4):
        finish(KV, chunk)
    send_pair(KV, 4)
    send_pair(KV, 5)
    finish(KV, 4)
    finish(KV, 5)

    def write_piece(at, result):
        slots[0, at, :] = result

    ordered(KV, write_piece)
    send(0, slot(1, 0, 0), 0, z_up)
    send(0, slot(2, 0, 0), 64, z_down)
    spread(0)

    send_far(Q, 4)
    send_far(Q, 5)
    for chunk in range(3):
        send_near(Q, chunk)
    step_y(0)
    step_z(1)
    step_z(2)
    for chunk in range(3, 6):
        send_near(Q, chunk)
    step_far(0)
    step_y(1)
    for chunk in range(3):
        send_pair(Q, chunk)
    step_z(3)
    step_y(2)
    step_far(1)
    for chunk in range(3):
        finish(Q, chunk)
    for chunk in range(3, 6):
        send_pair(Q, chunk)
    step_z(4)
    step_y(3)
    step_far(2)
    for chunk in range(3, 6):
        finish(Q, chunk)

    def write_queries(at, result):
        queries[at, :] = result

    ordered(Q, write_queries)
    step_z(5)

    own_pair = 1 + 2 * (1 - y_lo)
    unit(slot(0, y_lo * own_pair, 0), slot(0, (1 - y_lo) * own_pair, 0), 1, True)
    step_sibling(0)

    def stage_zero(part, carry):
        @pl.when(part < place)
        def _():
            part_hi, part_core = lax.div(part, 2), lax.rem(part, 2)
            other = lax.rem(part_core + core, 2)
            unit(
                slot(0, lax.rem(y - 2 * part_hi + NY, NY), other),
                slot(0, lax.rem(y - 2 * part_hi - 1 + NY, NY), other),
                1,
                False,
            )

        return carry

    lax.fori_loop(0, 3, stage_zero, 0)

    def later_stages(index, carry):
        stage, part_hi = lax.div(index, 2), lax.rem(index, 2)

        @pl.when(part_hi == 0)
        def _():
            @pl.when(stage + 5 < NZ)
            def _():
                step_z(stage + 5)

            @pl.when(stage + 3 < NZ)
            def _():
                step_y(stage + 3)

            @pl.when(stage + 2 < NZ)
            def _():
                step_far(stage + 2)

            step_sibling(stage)

        hops = lax.div(stage + 1, 2)
        odd = lax.rem(stage, 2)
        from_z = odd * (z - hops) + (1 - odd) * (z + hops - NZ)

        @pl.when(from_z >= 0)
        def _():
            unit(
                slot(stage, lax.rem(y - 2 * part_hi + NY, NY), 0),
                slot(stage, lax.rem(y - 2 * part_hi - 1 + NY, NY), 0),
                2,
                False,
            )

        return carry

    lax.fori_loop(2, 2 * NZ, later_stages, 0)

    for row in range(0, GRP, ROWS):
        for head in range(2):
            at = pl.ds(head * GRP + row, ROWS)
            out_ref[row : row + ROWS, head * HD : (head + 1) * HD] = (
                accum[at, :HD] / accum[at, HD:]
            ).astype(jnp.bfloat16)

    for each in copies:
        each.wait_send()
    slot_copy(0, 0, 64, sibling).wait_send()

    def settle(index, carry):
        stage, kind = lax.div(index, 8), lax.rem(index, 8)

        @pl.when((kind > 0) | (stage + 2 < NZ))
        def _():
            slot_copy(0, 0, index, sibling).wait_send()

        return carry

    lax.fori_loop(0, 8 * NZ, settle, 0)


def shards(
    frames,
    vis_gain,
    proj_weight,
    text_embed,
    text_lengths,
    norm_gain,
    q_weight,
    k_weight,
    v_weight,
    q_bias,
    k_bias,
    v_bias,
):
    bf16, f32 = jnp.bfloat16, jnp.float32
    inv_freq = np.power(1e6, -np.arange(HD // 2) * (2.0 / HD)).astype(np.float32)
    operands = (
        frames,
        vis_gain[None],
        proj_weight.T,
        text_embed.T,
        text_lengths,
        norm_gain[None],
        q_weight,
        k_weight,
        v_weight,
        q_bias[None],
        k_bias[None],
        v_bias[None],
        jnp.asarray(np.concatenate([inv_freq, inv_freq])[None]),
    )
    landing = [pltpu.VMEM(operand.shape, operand.dtype) for operand in operands]
    landing[4] = pltpu.SMEM(text_lengths.shape, text_lengths.dtype)
    features = text_embed.shape[1]
    sums = []
    for width in WIDTH:
        sums += [
            pltpu.VMEM((CHUNKS, CHUNK, width), bf16),
            pltpu.VMEM((CHUNKS, CHUNK, width), bf16),
            pltpu.VMEM((CHUNKS, 2, CHUNK, width), bf16),
            pltpu.VMEM((CHUNKS, 2, CHUNK, width), bf16),
            pltpu.VMEM((CHUNKS, CHUNK, width // 2), bf16),
            pltpu.VMEM((CHUNKS, CHUNK, width // 2), bf16),
            pltpu.VMEM((CHUNKS, CHUNK, width // 2), f32),
        ]
    return pl.pallas_call(
        kernel,
        out_shape=jax.ShapeDtypeStruct((GRP, 2 * HD), bf16),
        in_specs=[pl.BlockSpec(memory_space=pltpu.HBM)] * len(operands),
        out_specs=pl.BlockSpec(memory_space=pltpu.VMEM),
        scratch_shapes=landing
        + [
            pltpu.VMEM((2, 8, V), bf16),
            pltpu.VMEM((32, V), f32),
            pltpu.VMEM((8, 32, V), bf16),
            pltpu.VMEM((GRP, features), bf16),
            pltpu.VMEM((VIS_GRP, features), bf16),
            pltpu.VMEM((8, 8, TEXT_GRP), f32),
            pltpu.VMEM((8, 8, VIS_GRP), f32),
        ]
        + sums
        + [
            pltpu.VMEM((GRP, HD), f32),
            pltpu.VMEM((GRP, HD), f32),
            pltpu.VMEM((GRP, HD), bf16),
            pltpu.VMEM((GRP, 2 * HD), bf16),
            pltpu.VMEM((GRP, 2 * HD), bf16),
            pltpu.VMEM((8 * NZ, GRP, HD), bf16),
            pltpu.VMEM((2 * GRP, HD), f32),
            pltpu.VMEM((2 * GRP, 2 * HD), f32),
            pltpu.SemaphoreType.DMA((len(operands),)),
            pltpu.SemaphoreType.DMA((AT_SLOTS + 8 * NZ + 1,)),
            pltpu.SemaphoreType.DMA((AT_SLOTS + 8 * NZ,)),
        ],
        compiler_params=pltpu.CompilerParams(
            collective_id=0, has_side_effects=True, vmem_limit_bytes=56 * 1024 * 1024
        ),
        name="video_attention",
    )(*operands)


def solution(mesh):
    placed = (
        P("blk", "uly", None),
        P(),
        P(None, "uly"),
        P("blk", "uly"),
        P("blk", None),
        P("uly"),
        P("uly", None),
        P("uly", None),
        P("uly", None),
        P(),
        P(),
        P(),
    )
    return jax.shard_map(
        shards, mesh=mesh, in_specs=placed, out_specs=P("blk", "uly"), check_vma=False
    )
```

```python
import math

import jax
import jax.numpy as jnp
import numpy as np
from jax import lax
from jax.experimental import pallas as pl
from jax.experimental.pallas import tpu as pltpu
from jax.sharding import PartitionSpec as P

PATCH = 64
D = 3584
V = 1152
HD = 128
GRP = 768
TEXT_GRP = 512
VIS_GRP = 256
CHUNK = 128
CHUNKS = GRP // CHUNK
ROWS = 256
EXP2_SCALE = math.log2(math.e) / math.sqrt(HD)
NEG = -1e30
MESH = pl.DeviceIdType.MESH

NZ = 8
NY = 4

KV, Q = 0, 1
WIDTH = (2 * HD, 4 * HD)

AT_HALO, AT_TEXT, AT_VIS, AT_GATHER = 0, 0, 8, 16
AT_FAR, AT_NEAR, AT_PAIR = (24, 36), (48, 60), (72, 78)
AT_SLOTS = 84

SIDE = 256


def kernel(
    frames_hbm,
    vis_gain_hbm,
    proj_hbm,
    text_hbm,
    lengths_hbm,
    gain_hbm,
    wq_hbm,
    wk_hbm,
    wv_hbm,
    bq_hbm,
    bk_hbm,
    bv_hbm,
    freq_hbm,
    out_ref,
    frames_ref,
    vis_gain_ref,
    proj_ref,
    text_ref,
    lengths_ref,
    gain_ref,
    wq_ref,
    wk_ref,
    wv_ref,
    bq_ref,
    bk_ref,
    bv_ref,
    freq_ref,
    halo,
    normal_rows,
    gathered,
    rows,
    vis,
    text_sums,
    vis_sums,
    far_out_kv,
    far_in_kv,
    near_out_kv,
    near_in_kv,
    pair_out_kv,
    pair_in_kv,
    kept_kv,
    far_out_q,
    far_in_q,
    near_out_q,
    near_in_q,
    pair_out_q,
    pair_in_q,
    kept_q,
    cosine,
    sine,
    done_kv,
    done_q,
    queries,
    slots,
    top,
    accum,
    load_sem,
    send_sem,
    recv_sem,
):
    blk = lax.axis_index("blk")
    uly = lax.axis_index("uly")
    n_blk = lax.axis_size("blk")
    z, place = lax.div(blk, 4), lax.rem(blk, 4)
    y_hi, core = lax.div(place, 2), lax.rem(place, 2)
    x, y_lo = lax.div(uly, 2), lax.rem(uly, 2)
    y = 2 * y_hi + y_lo

    loads = [
        pltpu.make_async_copy(source, target, load_sem.at[number])
        for number, (source, target) in enumerate(
            (
                (frames_hbm, frames_ref),
                (text_hbm, text_ref),
                (vis_gain_hbm, vis_gain_ref),
                (gain_hbm, gain_ref),
                (wk_hbm, wk_ref),
                (wv_hbm, wv_ref),
                (proj_hbm, proj_ref),
                (lengths_hbm, lengths_ref),
                (freq_hbm, freq_ref),
                (bk_hbm, bk_ref),
                (bv_hbm, bv_ref),
                (bq_hbm, bq_ref),
                (wq_hbm, wq_ref),
            )
        )
    ]
    for load in loads:
        load.start()

    def device(z_at, y_at, core_at):
        return (z_at * 4 + lax.div(y_at, 2) * 2 + core_at, x * 2 + lax.rem(y_at, 2))

    z_up = device(lax.rem(z + 1, NZ), y, core)
    z_down = device(lax.rem(z + NZ - 1, NZ), y, core)
    y_up = device(z, lax.rem(y + 1, NY), core)
    y_down = device(z, lax.rem(y + NY - 1, NY), core)
    sibling = device(z, y, 1 - core)
    x_up, x_down, x_far = lax.rem(x + 1, 4), lax.rem(x + 3, 4), lax.rem(x + 2, 4)
    up, down, pair = (blk, x_up * 2 + y_lo), (blk, x_down * 2 + y_lo), (blk, x * 2 + 1 - y_lo)
    peers = [None] + [(blk, lax.rem(uly + step, 8)) for step in range(1, 8)]
    earlier = (lax.rem(blk + n_blk - 1, n_blk), uly)
    later = (lax.rem(blk + 1, n_blk), uly)

    barrier = pltpu.get_barrier_semaphore()
    others = peers[1:] + [earlier, later, z_up, z_down, y_up, y_down, sibling]
    for other in others:
        pl.semaphore_signal(barrier, inc=1, device_id=other, device_id_type=MESH)
    pl.semaphore_wait(barrier, len(others))

    copies = []

    def copy(source, target, sem, to):
        return pltpu.make_async_remote_copy(
            src_ref=source,
            dst_ref=target,
            send_sem=send_sem.at[sem],
            recv_sem=recv_sem.at[sem],
            device_id=to,
            device_id_type=MESH,
        )

    def start(each):
        each.start()
        copies.append(each)

    loads[0].wait()
    halo_copy = copy(frames_ref.at[0:2], halo, AT_HALO, earlier)
    start(halo_copy)

    def send_sums(sums, base):
        for step in range(1, 8):
            start(copy(sums.at[0], sums.at[step], base + step, peers[step]))

    def scales(sums, base):
        for step in range(1, 8):
            copy(sums.at[step], sums.at[step], base + step, peers[step]).wait_recv()
        total = sums[0]
        for step in range(1, 8):
            total = total + sums[step]
        return lax.rsqrt(total[0:1] / D + 1e-06)

    loads[1].wait()
    text = text_ref[...].astype(jnp.float32)
    text_sums[0] = jnp.broadcast_to(jnp.sum(text * text, 0, keepdims=True), (8, TEXT_GRP))
    send_sums(text_sums, AT_TEXT)

    for load in loads[2:6]:
        load.wait()
    halo_copy.wait_recv()
    tail = jnp.where(blk < n_blk - 1, halo[...].astype(jnp.float32), 0.0)
    frames = frames_ref[...].astype(jnp.float32)
    pairs = [frames[2 * i] + frames[2 * i + 1] for i in range(4)] + [tail[0] + tail[1]]
    for i in range(4):
        pooled = (pairs[i] + pairs[i + 1]) * 0.25
        centred = pooled - jnp.mean(pooled, -1, keepdims=True)
        variance = jnp.mean(centred * centred, -1, keepdims=True)
        normal_rows[8 * i : 8 * i + 8, :] = (
            centred * lax.rsqrt(variance + 1e-06) * vis_gain_ref[...]
        )
    gathered[uly] = normal_rows[...].astype(jnp.bfloat16)
    for step in range(1, 8):
        start(copy(gathered.at[uly], gathered.at[uly], AT_GATHER + step, peers[step]))

    scaled_text = jnp.transpose(text_ref[...].astype(jnp.float32) * scales(text_sums, AT_TEXT))
    rows[0:TEXT_GRP, :] = (scaled_text * gain_ref[...]).astype(jnp.bfloat16)

    far_out, far_in = (far_out_kv, far_out_q), (far_in_kv, far_in_q)
    near_out, near_in = (near_out_kv, near_out_q), (near_in_kv, near_in_q)
    pair_out, pair_in = (pair_out_kv, pair_out_q), (pair_in_kv, pair_in_q)
    kept, done = (kept_kv, kept_q), (done_kv, done_q)
    half = CHUNK // 2

    def partial(kind, chunk, x_at):
        left = rows[chunk * CHUNK : (chunk + 1) * CHUNK, :]
        if kind == Q:
            weight = wq_ref[:, pl.ds(pl.multiple_of(x_at * 4 * HD, 4 * HD), 4 * HD)]
            return jnp.dot(left, weight, preferred_element_type=jnp.float32)
        at = pl.ds(pl.multiple_of(x_at * HD, HD), HD)
        return jnp.concatenate(
            [
                jnp.dot(left, weight[:, at], preferred_element_type=jnp.float32)
                for weight in (wk_ref, wv_ref)
            ],
            1,
        )

    def far_copies(kind, chunk):
        out, into, base = far_out[kind].at[chunk], far_in[kind].at[chunk], AT_FAR[kind] + 2 * chunk
        return (
            copy(out.at[0:half], into.at[0:half], base, up),
            copy(out.at[half:CHUNK], into.at[half:CHUNK], base + 1, down),
        )

    def near_copies(kind, chunk):
        out, into = near_out[kind].at[chunk], near_in[kind].at[chunk]
        base = AT_NEAR[kind] + 2 * chunk
        return (
            copy(out.at[0], into.at[0], base, up),
            copy(out.at[1], into.at[1], base + 1, down),
        )

    def pair_copy(kind, chunk):
        return copy(
            pair_out[kind].at[chunk], pair_in[kind].at[chunk], AT_PAIR[kind] + chunk, pair
        )

    def send_far(kind, chunk):
        far_out[kind][chunk] = partial(kind, chunk, x_far).astype(jnp.bfloat16)
        for each in far_copies(kind, chunk):
            start(each)

    def send_near(kind, chunk):
        for each in far_copies(kind, chunk):
            each.wait_recv()
        for way, x_at in ((0, x_up), (1, x_down)):
            own = partial(kind, chunk, x_at)
            relayed = slice(way * half, way * half + half)
            rest = slice((1 - way) * half, (1 - way) * half + half)
            near_out[kind][chunk, way, relayed, :] = (
                own[relayed] + far_in[kind][chunk, relayed, :].astype(jnp.float32)
            ).astype(jnp.bfloat16)
            near_out[kind][chunk, way, rest, :] = own[rest].astype(jnp.bfloat16)
        for each in near_copies(kind, chunk):
            start(each)

    def send_pair(kind, chunk):
        for each in near_copies(kind, chunk):
            each.wait_recv()
        total = (
            partial(kind, chunk, x)
            + near_in[kind][chunk, 0].astype(jnp.float32)
            + near_in[kind][chunk, 1].astype(jnp.float32)
        )
        middle = WIDTH[kind] // 2
        low, high = total[:, :middle], total[:, middle:]
        kept[kind][chunk] = jnp.where(y_lo == 0, low, high)
        pair_out[kind][chunk] = jnp.where(y_lo == 0, high, low).astype(jnp.bfloat16)
        start(pair_copy(kind, chunk))

    def finish(kind, chunk):
        pair_copy(kind, chunk).wait_recv()
        at = slice(chunk * CHUNK, chunk * CHUNK + CHUNK)
        total = kept[kind][chunk] + pair_in[kind][chunk].astype(jnp.float32)
        if kind == KV:
            bias_at = pl.ds(pl.multiple_of(x * HD, HD), HD)
            total = total + jnp.where(y_lo == 0, bk_ref[:, bias_at], bv_ref[:, bias_at])
        else:
            total = total + bq_ref[:, pl.ds(pl.multiple_of(uly * 2 * HD, 2 * HD), 2 * HD)]
        for head in range(WIDTH[kind] // (2 * HD)):
            columns = slice(head * HD, head * HD + HD)
            plain = total[:, columns]
            turned = plain * cosine[at, :] + pltpu.roll(plain, HD // 2, 1) * sine[at, :]
            if kind == KV:
                turned = jnp.where(y_lo == 0, turned, plain)
            done[kind][at, columns] = turned.astype(jnp.bfloat16)

    def run_ends():
        ends = [lengths_ref[0, 0]]
        for run in range(1, 4):
            ends.append(ends[-1] + lengths_ref[0, run])
        return ends

    def text_places(index):
        place_of = index
        for end in run_ends():
            place_of = place_of + jnp.where(index >= end, PATCH, 0)
        return place_of

    def vis_places(index):
        frame = (index >> 3) & 3
        place_of = (index >> 5) * 8 + (index & 7)
        for number, end in enumerate(run_ends()):
            place_of = place_of + jnp.where(frame == number, end + PATCH * number, 0)
        return place_of

    def angles(first, count, places):
        index = lax.broadcasted_iota(jnp.int32, (count, HD), 0)
        angle = (blk * GRP + places(index)).astype(jnp.float32) * freq_ref[...]
        lane = lax.broadcasted_iota(jnp.int32, (count, HD), 1)
        cosine[first : first + count, :] = jnp.cos(angle)
        turned = jnp.sin(angle)
        sine[first : first + count, :] = jnp.where(lane < HD // 2, -turned, turned)

    def ordered(kind, write):
        index = lax.broadcasted_iota(jnp.int32, (CHUNK, TEXT_GRP), 1)
        vis_index = lax.broadcasted_iota(jnp.int32, (CHUNK, VIS_GRP), 1)
        places = jnp.concatenate([text_places(index), vis_places(vis_index)], 1)
        wanted = lax.broadcasted_iota(jnp.int32, (CHUNK, GRP), 0)
        for chunk in range(CHUNKS):
            chosen = jnp.where(places == wanted + chunk * CHUNK, 1.0, 0.0).astype(jnp.bfloat16)
            result = jnp.dot(chosen, done[kind][...], preferred_element_type=jnp.float32)
            write(slice(chunk * CHUNK, chunk * CHUNK + CHUNK), result.astype(jnp.bfloat16))

    def piece_copy(source, target, sem, landing, to):
        return pltpu.make_async_remote_copy(
            src_ref=source,
            dst_ref=target,
            send_sem=send_sem.at[AT_SLOTS + sem],
            recv_sem=recv_sem.at[AT_SLOTS + landing],
            device_id=to,
            device_id_type=MESH,
        )

    def front(stage, far):
        return slots.at[stage, 0, far, SIDE:GRP]

    def side(far):
        return slots.at[0, 0, far, 0:SIDE]

    def sides(stage):
        return slots.at[stage, 0, :, 0:SIDE]

    def send(source, target, sem, landing, to):
        piece_copy(source, target, sem, landing, to).start()

    def arrived(target, landing):
        piece_copy(target, target, 0, landing, sibling).wait_recv()

    def settled(source, sem):
        piece_copy(source, source, sem, 0, sibling).wait_send()

    def pass_z(stage, piece, sem, landing):
        odd = lax.rem(stage, 2) == 1

        @pl.when(odd & (stage + 2 < NZ))
        def _():
            send(piece(stage), piece(stage + 2), sem, landing, z_up)

        @pl.when(jnp.logical_not(odd) & (stage + 2 < NZ))
        def _():
            send(piece(stage), piece(stage + 2), sem, landing, z_down)

    def own_front(stage):
        return front(stage, 0)

    def to_neighbours(stage):
        send(front(stage, 0), front(stage, 1), stage * 8 + 1, stage * 4 + 1, y_up)
        send(front(stage, 0), front(stage, 3), stage * 8 + 2, stage * 4 + 3, y_down)

    def step_start():
        send(side(0), side(1), 66, 33, y_up)
        send(side(0), side(3), 67, 35, y_down)
        send(front(0, 0), front(1, 0), 0, 4, z_up)
        send(front(0, 0), front(2, 0), 64, 8, z_down)
        to_neighbours(0)

    def step_z(stage):
        arrived(front(stage, 0), stage * 4)
        pass_z(stage, own_front, stage * 8, (stage + 2) * 4)
        to_neighbours(stage)

    def step_y(stage):
        if isinstance(stage, int) and stage == 0:
            for far in (1, 3):
                arrived(side(far), 32 + far)
            send(side(1), side(2), 68, 34, y_up)
        else:
            arrived(sides(stage), 36 + stage)
            pass_z(stage, sides, stage * 8 + 4, 38 + stage)
        for far in (1, 3):
            arrived(front(stage, far), stage * 4 + far)
        odd = lax.rem(stage, 2) == 1

        @pl.when(odd)
        def _():
            send(front(stage, 3), front(stage, 2), stage * 8 + 3, stage * 4 + 2, y_down)

        @pl.when(jnp.logical_not(odd))
        def _():
            send(front(stage, 1), front(stage, 2), stage * 8 + 3, stage * 4 + 2, y_up)

    def step_far(stage):
        if isinstance(stage, int) and stage == 0:
            arrived(side(2), 34)
            send(sides(0), sides(1), 4, 37, z_up)
            send(sides(0), sides(2), 65, 38, z_down)
        arrived(front(stage, 2), stage * 4 + 2)
        send(slots.at[stage, 0], slots.at[stage, 1], stage * 8 + 5, 44 + stage, sibling)

    def step_sibling(stage):
        arrived(slots.at[stage, 1], 44 + stage)

    def block_of(where, count, last):
        stage, other, far = where
        if count == 1:
            return slots[stage, other, far, 0:last, :]
        return slots[stage, :, far].reshape(count * GRP, HD)

    def scores_of(keys, count, row, head, last):
        block = block_of(keys, count, last)
        return lax.dot_general(
            queries[row : row + ROWS, head * HD : (head + 1) * HD],
            block,
            (((1,), (1,)), ((), ())),
            preferred_element_type=jnp.float32,
        )

    def absorb(values, count, row, head, last, scores, first):
        at = pl.ds(head * GRP + row, ROWS)
        if first:
            query_at = lax.broadcasted_iota(jnp.int32, (ROWS, last), 0) + row
            key_at = lax.broadcasted_iota(jnp.int32, (ROWS, last), 1)
            scores = jnp.where(key_at <= query_at, scores, NEG)
        block_top = jnp.max(scores, 1, keepdims=True) * EXP2_SCALE
        if first:
            new_top = jnp.broadcast_to(block_top, (ROWS, HD))
        else:
            old_top = top[at, :]
            new_top = jnp.maximum(old_top, block_top)
        weights = jnp.exp2(scores * EXP2_SCALE - new_top[:, :1]).astype(jnp.bfloat16)
        block = block_of(values, count, last)
        gained = jnp.dot(
            weights,
            jnp.concatenate([block, jnp.ones(block.shape, jnp.bfloat16)], 1),
            preferred_element_type=jnp.float32,
        )
        top[at, :] = new_top
        if first:
            accum[at, :] = gained
        else:
            rescale = jnp.exp2(old_top - new_top)
            accum[at, :] = accum[at, :] * jnp.concatenate([rescale, rescale], 1) + gained

    def unit(keys, values, count, first):
        waiting = None
        for row in range(0, GRP, ROWS):
            for head in range(2):
                last = row + ROWS if first else GRP
                scores = scores_of(keys, count, row, head, last)
                if waiting is not None:
                    absorb(values, count, *waiting, first)
                waiting = (row, head, last, scores)
        absorb(values, count, *waiting, first)

    for chunk in range(4):
        send_far(KV, chunk)
    loads[6].wait()
    for step in range(1, 8):
        source = lax.rem(uly + 8 - step, 8)
        copy(gathered.at[source], gathered.at[source], AT_GATHER + step, peers[step]).wait_recv()
    vis[...] = lax.dot_general(
        gathered[...].reshape(VIS_GRP, V),
        proj_ref[...],
        (((1,), (1,)), ((), ())),
        preferred_element_type=jnp.float32,
    ).astype(jnp.bfloat16)
    vis_float = vis[...].astype(jnp.float32)
    squares = jnp.sum(vis_float * vis_float, 1, keepdims=True)
    vis_sums[0] = jnp.transpose(jnp.broadcast_to(squares, (VIS_GRP, 128)))[0:8]
    send_sums(vis_sums, AT_VIS)
    for chunk in range(4):
        send_near(KV, chunk)
    inverse = jnp.transpose(jnp.broadcast_to(scales(vis_sums, AT_VIS), (128, VIS_GRP)))[:, 0:1]
    rows[TEXT_GRP:GRP, :] = (vis[...].astype(jnp.float32) * inverse * gain_ref[...]).astype(
        jnp.bfloat16
    )
    send_far(KV, 4)
    send_far(KV, 5)
    for load in loads[7:]:
        load.wait()
    for chunk in range(4):
        send_far(Q, chunk)
    angles(0, TEXT_GRP, text_places)
    send_near(KV, 4)
    send_near(KV, 5)
    for chunk in range(4):
        send_pair(KV, chunk)
    angles(TEXT_GRP, VIS_GRP, vis_places)
    for chunk in range(4):
        finish(KV, chunk)
    send_pair(KV, 4)
    send_pair(KV, 5)
    finish(KV, 4)
    finish(KV, 5)

    def write_piece(at, result):
        slots[0, 0, 0, at, :] = result

    ordered(KV, write_piece)
    step_start()

    send_far(Q, 4)
    send_far(Q, 5)
    for chunk in range(3):
        send_near(Q, chunk)
    step_y(0)
    step_z(1)
    step_z(2)
    for chunk in range(3, 6):
        send_near(Q, chunk)
    step_far(0)
    step_y(1)
    for chunk in range(3):
        send_pair(Q, chunk)
    step_z(3)
    step_y(2)
    step_far(1)
    for chunk in range(3):
        finish(Q, chunk)
    for chunk in range(3, 6):
        send_pair(Q, chunk)
    step_z(4)
    step_y(3)
    step_far(2)
    for chunk in range(3, 6):
        finish(Q, chunk)

    def write_queries(at, result):
        queries[at, :] = result

    ordered(Q, write_queries)
    step_z(5)

    own_pair = 1 + 2 * (1 - y_lo)
    unit((0, 0, y_lo * own_pair), (0, 0, (1 - y_lo) * own_pair), 1, True)
    step_sibling(0)

    def stage_zero(part, carry):
        @pl.when(part < place)
        def _():
            part_hi, part_core = lax.div(part, 2), lax.rem(part, 2)
            other = lax.rem(part_core + core, 2)
            unit(
                (0, other, lax.rem(y - 2 * part_hi + NY, NY)),
                (0, other, lax.rem(y - 2 * part_hi - 1 + NY, NY)),
                1,
                False,
            )

        return carry

    lax.fori_loop(0, 3, stage_zero, 0)

    def later_stages(index, carry):
        stage, part_hi = lax.div(index, 2), lax.rem(index, 2)

        @pl.when(part_hi == 0)
        def _():
            @pl.when(stage + 5 < NZ)
            def _():
                step_z(stage + 5)

            @pl.when(stage + 3 < NZ)
            def _():
                step_y(stage + 3)

            @pl.when(stage + 2 < NZ)
            def _():
                step_far(stage + 2)

            step_sibling(stage)

        hops = lax.div(stage + 1, 2)
        odd = lax.rem(stage, 2)
        from_z = odd * (z - hops) + (1 - odd) * (z + hops - NZ)

        @pl.when(from_z >= 0)
        def _():
            unit(
                (stage, 0, lax.rem(y - 2 * part_hi + NY, NY)),
                (stage, 0, lax.rem(y - 2 * part_hi - 1 + NY, NY)),
                2,
                False,
            )

        return carry

    lax.fori_loop(2, 2 * NZ, later_stages, 0)

    for row in range(0, GRP, ROWS):
        for head in range(2):
            at = pl.ds(head * GRP + row, ROWS)
            out_ref[row : row + ROWS, head * HD : (head + 1) * HD] = (
                accum[at, :HD] / accum[at, HD:]
            ).astype(jnp.bfloat16)

    for each in copies:
        each.wait_send()
    settled(front(0, 0), 64)
    settled(sides(0), 65)
    for step in range(3):
        settled(side(0), 66 + step)

    def settle(stage, carry):
        for kind in range(1, 4):
            settled(front(0, 0), stage * 8 + kind)
        settled(slots.at[0, 0], stage * 8 + 5)

        @pl.when(stage + 2 < NZ)
        def _():
            settled(front(0, 0), stage * 8)
            settled(sides(0), stage * 8 + 4)

        return carry

    lax.fori_loop(0, NZ, settle, 0)


def shards(
    frames,
    vis_gain,
    proj_weight,
    text_embed,
    text_lengths,
    norm_gain,
    q_weight,
    k_weight,
    v_weight,
    q_bias,
    k_bias,
    v_bias,
):
    bf16, f32 = jnp.bfloat16, jnp.float32
    inv_freq = np.power(1e6, -np.arange(HD // 2) * (2.0 / HD)).astype(np.float32)
    operands = (
        frames,
        vis_gain[None],
        proj_weight.T,
        text_embed.T,
        text_lengths,
        norm_gain[None],
        q_weight,
        k_weight,
        v_weight,
        q_bias[None],
        k_bias[None],
        v_bias[None],
        jnp.asarray(np.concatenate([inv_freq, inv_freq])[None]),
    )
    landing = [pltpu.VMEM(operand.shape, operand.dtype) for operand in operands]
    landing[4] = pltpu.SMEM(text_lengths.shape, text_lengths.dtype)
    features = text_embed.shape[1]
    sums = []
    for width in WIDTH:
        sums += [
            pltpu.VMEM((CHUNKS, CHUNK, width), bf16),
            pltpu.VMEM((CHUNKS, CHUNK, width), bf16),
            pltpu.VMEM((CHUNKS, 2, CHUNK, width), bf16),
            pltpu.VMEM((CHUNKS, 2, CHUNK, width), bf16),
            pltpu.VMEM((CHUNKS, CHUNK, width // 2), bf16),
            pltpu.VMEM((CHUNKS, CHUNK, width // 2), bf16),
            pltpu.VMEM((CHUNKS, CHUNK, width // 2), f32),
        ]
    return pl.pallas_call(
        kernel,
        out_shape=jax.ShapeDtypeStruct((GRP, 2 * HD), bf16),
        in_specs=[pl.BlockSpec(memory_space=pltpu.HBM)] * len(operands),
        out_specs=pl.BlockSpec(memory_space=pltpu.VMEM),
        scratch_shapes=landing
        + [
            pltpu.VMEM((2, 8, V), bf16),
            pltpu.VMEM((32, V), f32),
            pltpu.VMEM((8, 32, V), bf16),
            pltpu.VMEM((GRP, features), bf16),
            pltpu.VMEM((VIS_GRP, features), bf16),
            pltpu.VMEM((8, 8, TEXT_GRP), f32),
            pltpu.VMEM((8, 8, VIS_GRP), f32),
        ]
        + sums
        + [
            pltpu.VMEM((GRP, HD), f32),
            pltpu.VMEM((GRP, HD), f32),
            pltpu.VMEM((GRP, HD), bf16),
            pltpu.VMEM((GRP, 2 * HD), bf16),
            pltpu.VMEM((GRP, 2 * HD), bf16),
            pltpu.VMEM((NZ, 2, NY, GRP, HD), bf16),
            pltpu.VMEM((2 * GRP, HD), f32),
            pltpu.VMEM((2 * GRP, 2 * HD), f32),
            pltpu.SemaphoreType.DMA((len(operands),)),
            pltpu.SemaphoreType.DMA((AT_SLOTS + 69,)),
            pltpu.SemaphoreType.DMA((AT_SLOTS + 52,)),
        ],
        compiler_params=pltpu.CompilerParams(
            collective_id=0, has_side_effects=True, vmem_limit_bytes=56 * 1024 * 1024
        ),
        name="video_attention",
    )(*operands)


def solution(mesh):
    placed = (
        P("blk", "uly", None),
        P(),
        P(None, "uly"),
        P("blk", "uly"),
        P("blk", None),
        P("uly"),
        P("uly", None),
        P("uly", None),
        P("uly", None),
        P(),
        P(),
        P(),
    )
    return jax.shard_map(
        shards, mesh=mesh, in_specs=placed, out_specs=P("blk", "uly"), check_vma=False
    )
```

```python
import math

import jax
import jax.numpy as jnp
import numpy as np
from jax import lax
from jax.experimental import pallas as pl
from jax.experimental.pallas import tpu as pltpu
from jax.sharding import PartitionSpec as P

PATCH = 64
D = 3584
V = 1152
HD = 128
GRP = 768
TEXT_GRP = 512
VIS_GRP = 256
CHUNK = 128
CHUNKS = GRP // CHUNK
ROWS = 256
EXP2_SCALE = math.log2(math.e) / math.sqrt(HD)
NEG = -1e30
MESH = pl.DeviceIdType.MESH

NZ = 8
NY = 4

KV, Q = 0, 1
WIDTH = (2 * HD, 4 * HD)

AT_HALO, AT_TEXT, AT_VIS, AT_GATHER = 0, 0, 8, 16
AT_FAR, AT_NEAR, AT_PAIR = (24, 36), (48, 60), (72, 78)
AT_SLOTS = 84

SIDE = 256


def kernel(
    frames_hbm,
    vis_gain_hbm,
    proj_hbm,
    text_hbm,
    lengths_hbm,
    gain_hbm,
    wq_hbm,
    wk_hbm,
    wv_hbm,
    bq_hbm,
    bk_hbm,
    bv_hbm,
    freq_hbm,
    out_ref,
    frames_ref,
    vis_gain_ref,
    proj_ref,
    text_ref,
    lengths_ref,
    gain_ref,
    wq_ref,
    wk_ref,
    wv_ref,
    bq_ref,
    bk_ref,
    bv_ref,
    freq_ref,
    halo,
    normal_rows,
    gathered,
    rows,
    vis,
    text_sums,
    vis_sums,
    far_out_kv,
    far_in_kv,
    near_out_kv,
    near_in_kv,
    pair_out_kv,
    pair_in_kv,
    kept_kv,
    far_out_q,
    far_in_q,
    near_out_q,
    near_in_q,
    pair_out_q,
    pair_in_q,
    kept_q,
    cosine,
    sine,
    done_kv,
    done_q,
    queries,
    slots,
    top,
    accum,
    load_sem,
    send_sem,
    recv_sem,
):
    blk = lax.axis_index("blk")
    uly = lax.axis_index("uly")
    n_blk = lax.axis_size("blk")
    z, place = lax.div(blk, 4), lax.rem(blk, 4)
    y_hi, core = lax.div(place, 2), lax.rem(place, 2)
    x, y_lo = lax.div(uly, 2), lax.rem(uly, 2)
    y = 2 * y_hi + y_lo

    loads = [
        pltpu.make_async_copy(source, target, load_sem.at[number])
        for number, (source, target) in enumerate(
            (
                (frames_hbm, frames_ref),
                (text_hbm, text_ref),
                (vis_gain_hbm, vis_gain_ref),
                (gain_hbm, gain_ref),
                (wk_hbm, wk_ref),
                (wv_hbm, wv_ref),
                (proj_hbm, proj_ref),
                (lengths_hbm, lengths_ref),
                (freq_hbm, freq_ref),
                (bk_hbm, bk_ref),
                (bv_hbm, bv_ref),
                (bq_hbm, bq_ref),
                (wq_hbm, wq_ref),
            )
        )
    ]
    for load in loads:
        load.start()

    def device(z_at, y_at, core_at):
        return (z_at * 4 + lax.div(y_at, 2) * 2 + core_at, x * 2 + lax.rem(y_at, 2))

    z_up = device(lax.rem(z + 1, NZ), y, core)
    z_down = device(lax.rem(z + NZ - 1, NZ), y, core)
    y_up = device(z, lax.rem(y + 1, NY), core)
    y_down = device(z, lax.rem(y + NY - 1, NY), core)
    sibling = device(z, y, 1 - core)
    x_up, x_down, x_far = lax.rem(x + 1, 4), lax.rem(x + 3, 4), lax.rem(x + 2, 4)
    up, down, pair = (blk, x_up * 2 + y_lo), (blk, x_down * 2 + y_lo), (blk, x * 2 + 1 - y_lo)
    peers = [None] + [(blk, lax.rem(uly + step, 8)) for step in range(1, 8)]
    earlier = (lax.rem(blk + n_blk - 1, n_blk), uly)
    later = (lax.rem(blk + 1, n_blk), uly)

    barrier = pltpu.get_barrier_semaphore()
    others = peers[1:] + [earlier, later, z_up, z_down, y_up, y_down, sibling]
    for other in others:
        pl.semaphore_signal(barrier, inc=1, device_id=other, device_id_type=MESH)
    pl.semaphore_wait(barrier, len(others))

    copies = []

    def copy(source, target, sem, to):
        return pltpu.make_async_remote_copy(
            src_ref=source,
            dst_ref=target,
            send_sem=send_sem.at[sem],
            recv_sem=recv_sem.at[sem],
            device_id=to,
            device_id_type=MESH,
        )

    def start(each):
        each.start()
        copies.append(each)

    loads[0].wait()
    halo_copy = copy(frames_ref.at[0:2], halo, AT_HALO, earlier)
    start(halo_copy)

    def send_sums(sums, base):
        for step in range(1, 8):
            start(copy(sums.at[0], sums.at[step], base + step, peers[step]))

    def scales(sums, base):
        for step in range(1, 8):
            copy(sums.at[step], sums.at[step], base + step, peers[step]).wait_recv()
        total = sums[0]
        for step in range(1, 8):
            total = total + sums[step]
        return lax.rsqrt(total[0:1] / D + 1e-06)

    loads[1].wait()
    text = text_ref[...].astype(jnp.float32)
    text_sums[0] = jnp.broadcast_to(jnp.sum(text * text, 0, keepdims=True), (8, TEXT_GRP))
    send_sums(text_sums, AT_TEXT)

    for load in loads[2:6]:
        load.wait()
    halo_copy.wait_recv()
    tail = jnp.where(blk < n_blk - 1, halo[...].astype(jnp.float32), 0.0)
    frames = frames_ref[...].astype(jnp.float32)
    pairs = [frames[2 * i] + frames[2 * i + 1] for i in range(4)] + [tail[0] + tail[1]]
    for i in range(4):
        pooled = (pairs[i] + pairs[i + 1]) * 0.25
        centred = pooled - jnp.mean(pooled, -1, keepdims=True)
        variance = jnp.mean(centred * centred, -1, keepdims=True)
        normal_rows[8 * i : 8 * i + 8, :] = (
            centred * lax.rsqrt(variance + 1e-06) * vis_gain_ref[...]
        )
    gathered[uly] = normal_rows[...].astype(jnp.bfloat16)
    for step in range(1, 8):
        start(copy(gathered.at[uly], gathered.at[uly], AT_GATHER + step, peers[step]))

    scaled_text = jnp.transpose(text_ref[...].astype(jnp.float32) * scales(text_sums, AT_TEXT))
    rows[0:TEXT_GRP, :] = (scaled_text * gain_ref[...]).astype(jnp.bfloat16)

    far_out, far_in = (far_out_kv, far_out_q), (far_in_kv, far_in_q)
    near_out, near_in = (near_out_kv, near_out_q), (near_in_kv, near_in_q)
    pair_out, pair_in = (pair_out_kv, pair_out_q), (pair_in_kv, pair_in_q)
    kept, done = (kept_kv, kept_q), (done_kv, done_q)
    half = CHUNK // 2

    def partial(kind, chunk, x_at):
        left = rows[chunk * CHUNK : (chunk + 1) * CHUNK, :]
        if kind == Q:
            weight = wq_ref[:, pl.ds(pl.multiple_of(x_at * 4 * HD, 4 * HD), 4 * HD)]
            return jnp.dot(left, weight, preferred_element_type=jnp.float32)
        at = pl.ds(pl.multiple_of(x_at * HD, HD), HD)
        return jnp.concatenate(
            [
                jnp.dot(left, weight[:, at], preferred_element_type=jnp.float32)
                for weight in (wk_ref, wv_ref)
            ],
            1,
        )

    def far_copies(kind, chunk):
        out, into, base = far_out[kind].at[chunk], far_in[kind].at[chunk], AT_FAR[kind] + 2 * chunk
        return (
            copy(out.at[0:half], into.at[0:half], base, up),
            copy(out.at[half:CHUNK], into.at[half:CHUNK], base + 1, down),
        )

    def near_copies(kind, chunk):
        out, into = near_out[kind].at[chunk], near_in[kind].at[chunk]
        base = AT_NEAR[kind] + 2 * chunk
        return (
            copy(out.at[0], into.at[0], base, up),
            copy(out.at[1], into.at[1], base + 1, down),
        )

    def pair_copy(kind, chunk):
        return copy(
            pair_out[kind].at[chunk], pair_in[kind].at[chunk], AT_PAIR[kind] + chunk, pair
        )

    def send_far(kind, chunk):
        far_out[kind][chunk] = partial(kind, chunk, x_far).astype(jnp.bfloat16)
        for each in far_copies(kind, chunk):
            start(each)

    def send_near(kind, chunk):
        for each in far_copies(kind, chunk):
            each.wait_recv()
        for way, x_at in ((0, x_up), (1, x_down)):
            own = partial(kind, chunk, x_at)
            relayed = slice(way * half, way * half + half)
            rest = slice((1 - way) * half, (1 - way) * half + half)
            near_out[kind][chunk, way, relayed, :] = (
                own[relayed] + far_in[kind][chunk, relayed, :].astype(jnp.float32)
            ).astype(jnp.bfloat16)
            near_out[kind][chunk, way, rest, :] = own[rest].astype(jnp.bfloat16)
        for each in near_copies(kind, chunk):
            start(each)

    def send_pair(kind, chunk):
        for each in near_copies(kind, chunk):
            each.wait_recv()
        total = (
            partial(kind, chunk, x)
            + near_in[kind][chunk, 0].astype(jnp.float32)
            + near_in[kind][chunk, 1].astype(jnp.float32)
        )
        middle = WIDTH[kind] // 2
        low, high = total[:, :middle], total[:, middle:]
        kept[kind][chunk] = jnp.where(y_lo == 0, low, high)
        pair_out[kind][chunk] = jnp.where(y_lo == 0, high, low).astype(jnp.bfloat16)
        start(pair_copy(kind, chunk))

    def finish(kind, chunk):
        pair_copy(kind, chunk).wait_recv()
        at = slice(chunk * CHUNK, chunk * CHUNK + CHUNK)
        total = kept[kind][chunk] + pair_in[kind][chunk].astype(jnp.float32)
        if kind == KV:
            bias_at = pl.ds(pl.multiple_of(x * HD, HD), HD)
            total = total + jnp.where(y_lo == 0, bk_ref[:, bias_at], bv_ref[:, bias_at])
        else:
            total = total + bq_ref[:, pl.ds(pl.multiple_of(uly * 2 * HD, 2 * HD), 2 * HD)]
        for head in range(WIDTH[kind] // (2 * HD)):
            columns = slice(head * HD, head * HD + HD)
            plain = total[:, columns]
            turned = plain * cosine[at, :] + pltpu.roll(plain, HD // 2, 1) * sine[at, :]
            if kind == KV:
                turned = jnp.where(y_lo == 0, turned, plain)
            done[kind][at, columns] = turned.astype(jnp.bfloat16)

    def run_ends():
        ends = [lengths_ref[0, 0]]
        for run in range(1, 4):
            ends.append(ends[-1] + lengths_ref[0, run])
        return ends

    def text_places(index):
        place_of = index
        for end in run_ends():
            place_of = place_of + jnp.where(index >= end, PATCH, 0)
        return place_of

    def vis_places(index):
        frame = (index >> 3) & 3
        place_of = (index >> 5) * 8 + (index & 7)
        for number, end in enumerate(run_ends()):
            place_of = place_of + jnp.where(frame == number, end + PATCH * number, 0)
        return place_of

    def angles(first, count, places):
        index = lax.broadcasted_iota(jnp.int32, (count, HD), 0)
        angle = (blk * GRP + places(index)).astype(jnp.float32) * freq_ref[...]
        lane = lax.broadcasted_iota(jnp.int32, (count, HD), 1)
        cosine[first : first + count, :] = jnp.cos(angle)
        turned = jnp.sin(angle)
        sine[first : first + count, :] = jnp.where(lane < HD // 2, -turned, turned)

    def ordered(kind, write):
        index = lax.broadcasted_iota(jnp.int32, (CHUNK, TEXT_GRP), 1)
        vis_index = lax.broadcasted_iota(jnp.int32, (CHUNK, VIS_GRP), 1)
        places = jnp.concatenate([text_places(index), vis_places(vis_index)], 1)
        wanted = lax.broadcasted_iota(jnp.int32, (CHUNK, GRP), 0)
        for chunk in range(CHUNKS):
            chosen = jnp.where(places == wanted + chunk * CHUNK, 1.0, 0.0).astype(jnp.bfloat16)
            result = jnp.dot(chosen, done[kind][...], preferred_element_type=jnp.float32)
            write(slice(chunk * CHUNK, chunk * CHUNK + CHUNK), result.astype(jnp.bfloat16))

    def piece_copy(source, target, sem, landing, to):
        return pltpu.make_async_remote_copy(
            src_ref=source,
            dst_ref=target,
            send_sem=send_sem.at[AT_SLOTS + sem],
            recv_sem=recv_sem.at[AT_SLOTS + landing],
            device_id=to,
            device_id_type=MESH,
        )

    def front(stage, far):
        return slots.at[stage, 0, far, SIDE:GRP]

    def side(far):
        return slots.at[0, 0, far, 0:SIDE]

    def sides(stage):
        return slots.at[stage, 0, :, 0:SIDE]

    def send(source, target, sem, landing, to):
        piece_copy(source, target, sem, landing, to).start()

    def arrived(target, landing):
        piece_copy(target, target, 0, landing, sibling).wait_recv()

    def settled(source, sem):
        piece_copy(source, source, sem, 0, sibling).wait_send()

    def pass_z(stage, piece, sem, landing):
        odd = lax.rem(stage, 2) == 1

        @pl.when(odd & (stage + 2 < NZ))
        def _():
            send(piece(stage), piece(stage + 2), sem, landing, z_up)

        @pl.when(jnp.logical_not(odd) & (stage + 2 < NZ))
        def _():
            send(piece(stage), piece(stage + 2), sem, landing, z_down)

    def own_front(stage):
        return front(stage, 0)

    def to_neighbours(stage):
        send(front(stage, 0), front(stage, 1), stage * 8 + 1, stage * 4 + 1, y_up)
        send(front(stage, 0), front(stage, 3), stage * 8 + 2, stage * 4 + 3, y_down)

    def step_start():
        send(side(0), side(1), 66, 33, y_up)
        send(side(0), side(3), 67, 35, y_down)
        send(front(0, 0), front(1, 0), 0, 4, z_up)
        send(front(0, 0), front(2, 0), 64, 8, z_down)
        to_neighbours(0)

    def step_z(stage):
        arrived(front(stage, 0), stage * 4)
        pass_z(stage, own_front, stage * 8, (stage + 2) * 4)
        to_neighbours(stage)

    def step_y(stage):
        if isinstance(stage, int) and stage == 0:
            for far in (1, 3):
                arrived(side(far), 32 + far)
            send(side(1), side(2), 68, 34, y_up)
        else:
            arrived(sides(stage), 36 + stage)
            pass_z(stage, sides, stage * 8 + 4, 38 + stage)
        for far in (1, 3):
            arrived(front(stage, far), stage * 4 + far)
        odd = lax.rem(stage, 2) == 1

        @pl.when(odd)
        def _():
            send(front(stage, 3), front(stage, 2), stage * 8 + 3, stage * 4 + 2, y_down)

        @pl.when(jnp.logical_not(odd))
        def _():
            send(front(stage, 1), front(stage, 2), stage * 8 + 3, stage * 4 + 2, y_up)

    def step_far(stage):
        if isinstance(stage, int) and stage == 0:
            arrived(side(2), 34)
            send(sides(0), sides(1), 4, 37, z_up)
            send(sides(0), sides(2), 65, 38, z_down)
        arrived(front(stage, 2), stage * 4 + 2)
        send(slots.at[stage, 0], slots.at[stage, 1], stage * 8 + 5, 44 + stage, sibling)

    def step_sibling(stage):
        arrived(slots.at[stage, 1], 44 + stage)

    def block_of(where, count, last):
        stage, other, far = where
        if count == 1:
            return slots[stage, other, far, 0:last, :]
        beyond = lax.rem(far + 2, NY)
        return jnp.concatenate(
            [slots[stage, :, at].reshape(2 * GRP, HD) for at in (far, beyond)], 0
        )

    def scores_of(keys, count, row, head, last):
        block = block_of(keys, count, last)
        return lax.dot_general(
            queries[row : row + ROWS, head * HD : (head + 1) * HD],
            block,
            (((1,), (1,)), ((), ())),
            preferred_element_type=jnp.float32,
        )

    def absorb(values, count, row, head, last, scores, first):
        at = pl.ds(head * GRP + row, ROWS)
        if first:
            query_at = lax.broadcasted_iota(jnp.int32, (ROWS, last), 0) + row
            key_at = lax.broadcasted_iota(jnp.int32, (ROWS, last), 1)
            scores = jnp.where(key_at <= query_at, scores, NEG)
        block_top = jnp.max(scores, 1, keepdims=True) * EXP2_SCALE
        if first:
            new_top = jnp.broadcast_to(block_top, (ROWS, HD))
        else:
            old_top = top[at, :]
            new_top = jnp.maximum(old_top, block_top)
        weights = jnp.exp2(scores * EXP2_SCALE - new_top[:, :1]).astype(jnp.bfloat16)
        block = block_of(values, count, last)
        gained = jnp.dot(
            weights,
            jnp.concatenate([block, jnp.ones(block.shape, jnp.bfloat16)], 1),
            preferred_element_type=jnp.float32,
        )
        top[at, :] = new_top
        if first:
            accum[at, :] = gained
        else:
            rescale = jnp.exp2(old_top - new_top)
            accum[at, :] = accum[at, :] * jnp.concatenate([rescale, rescale], 1) + gained

    def unit(keys, values, count, first):
        waiting = None
        for row in range(0, GRP, ROWS):
            for head in range(2):
                last = row + ROWS if first else GRP
                scores = scores_of(keys, count, row, head, last)
                if waiting is not None:
                    absorb(values, count, *waiting, first)
                waiting = (row, head, last, scores)
        absorb(values, count, *waiting, first)

    for chunk in range(4):
        send_far(KV, chunk)
    loads[6].wait()
    for step in range(1, 8):
        source = lax.rem(uly + 8 - step, 8)
        copy(gathered.at[source], gathered.at[source], AT_GATHER + step, peers[step]).wait_recv()
    vis[...] = lax.dot_general(
        gathered[...].reshape(VIS_GRP, V),
        proj_ref[...],
        (((1,), (1,)), ((), ())),
        preferred_element_type=jnp.float32,
    ).astype(jnp.bfloat16)
    vis_float = vis[...].astype(jnp.float32)
    squares = jnp.sum(vis_float * vis_float, 1, keepdims=True)
    vis_sums[0] = jnp.transpose(jnp.broadcast_to(squares, (VIS_GRP, 128)))[0:8]
    send_sums(vis_sums, AT_VIS)
    for chunk in range(4):
        send_near(KV, chunk)
    inverse = jnp.transpose(jnp.broadcast_to(scales(vis_sums, AT_VIS), (128, VIS_GRP)))[:, 0:1]
    rows[TEXT_GRP:GRP, :] = (vis[...].astype(jnp.float32) * inverse * gain_ref[...]).astype(
        jnp.bfloat16
    )
    send_far(KV, 4)
    send_far(KV, 5)
    for load in loads[7:]:
        load.wait()
    for chunk in range(4):
        send_far(Q, chunk)
    angles(0, TEXT_GRP, text_places)
    send_near(KV, 4)
    send_near(KV, 5)
    for chunk in range(4):
        send_pair(KV, chunk)
    angles(TEXT_GRP, VIS_GRP, vis_places)
    for chunk in range(4):
        finish(KV, chunk)
    send_pair(KV, 4)
    send_pair(KV, 5)
    finish(KV, 4)
    finish(KV, 5)

    def write_piece(at, result):
        slots[0, 0, 0, at, :] = result

    ordered(KV, write_piece)
    step_start()

    send_far(Q, 4)
    send_far(Q, 5)
    for chunk in range(3):
        send_near(Q, chunk)
    step_y(0)
    step_z(1)
    step_z(2)
    for chunk in range(3, 6):
        send_near(Q, chunk)
    step_far(0)
    step_y(1)
    for chunk in range(3):
        send_pair(Q, chunk)
    step_z(3)
    step_y(2)
    step_far(1)
    for chunk in range(3):
        finish(Q, chunk)
    for chunk in range(3, 6):
        send_pair(Q, chunk)
    step_z(4)
    step_y(3)
    step_far(2)
    for chunk in range(3, 6):
        finish(Q, chunk)

    def write_queries(at, result):
        queries[at, :] = result

    ordered(Q, write_queries)
    step_z(5)

    own_pair = 1 + 2 * (1 - y_lo)
    unit((0, 0, y_lo * own_pair), (0, 0, (1 - y_lo) * own_pair), 1, True)
    step_sibling(0)

    def stage_zero(part, carry):
        @pl.when(part < place)
        def _():
            part_hi, part_core = lax.div(part, 2), lax.rem(part, 2)
            other = lax.rem(part_core + core, 2)
            unit(
                (0, other, lax.rem(y - 2 * part_hi + NY, NY)),
                (0, other, lax.rem(y - 2 * part_hi - 1 + NY, NY)),
                1,
                False,
            )

        return carry

    lax.fori_loop(0, 3, stage_zero, 0)

    def later_stages(stage, carry):
        @pl.when(stage + 5 < NZ)
        def _():
            step_z(stage + 5)

        @pl.when(stage + 3 < NZ)
        def _():
            step_y(stage + 3)

        @pl.when(stage + 2 < NZ)
        def _():
            step_far(stage + 2)

        step_sibling(stage)

        hops = lax.div(stage + 1, 2)
        odd = lax.rem(stage, 2)
        from_z = odd * (z - hops) + (1 - odd) * (z + hops - NZ)

        @pl.when(from_z >= 0)
        def _():
            unit((stage, 0, y), (stage, 0, lax.rem(y + NY - 1, NY)), 4, False)

        return carry

    lax.fori_loop(1, NZ, later_stages, 0)

    for row in range(0, GRP, ROWS):
        for head in range(2):
            at = pl.ds(head * GRP + row, ROWS)
            out_ref[row : row + ROWS, head * HD : (head + 1) * HD] = (
                accum[at, :HD] / accum[at, HD:]
            ).astype(jnp.bfloat16)

    for each in copies:
        each.wait_send()
    settled(front(0, 0), 64)
    settled(sides(0), 65)
    for step in range(3):
        settled(side(0), 66 + step)

    def settle(stage, carry):
        for kind in range(1, 4):
            settled(front(0, 0), stage * 8 + kind)
        settled(slots.at[0, 0], stage * 8 + 5)

        @pl.when(stage + 2 < NZ)
        def _():
            settled(front(0, 0), stage * 8)
            settled(sides(0), stage * 8 + 4)

        return carry

    lax.fori_loop(0, NZ, settle, 0)


def shards(
    frames,
    vis_gain,
    proj_weight,
    text_embed,
    text_lengths,
    norm_gain,
    q_weight,
    k_weight,
    v_weight,
    q_bias,
    k_bias,
    v_bias,
):
    bf16, f32 = jnp.bfloat16, jnp.float32
    inv_freq = np.power(1e6, -np.arange(HD // 2) * (2.0 / HD)).astype(np.float32)
    operands = (
        frames,
        vis_gain[None],
        proj_weight.T,
        text_embed.T,
        text_lengths,
        norm_gain[None],
        q_weight,
        k_weight,
        v_weight,
        q_bias[None],
        k_bias[None],
        v_bias[None],
        jnp.asarray(np.concatenate([inv_freq, inv_freq])[None]),
    )
    landing = [pltpu.VMEM(operand.shape, operand.dtype) for operand in operands]
    landing[4] = pltpu.SMEM(text_lengths.shape, text_lengths.dtype)
    features = text_embed.shape[1]
    sums = []
    for width in WIDTH:
        sums += [
            pltpu.VMEM((CHUNKS, CHUNK, width), bf16),
            pltpu.VMEM((CHUNKS, CHUNK, width), bf16),
            pltpu.VMEM((CHUNKS, 2, CHUNK, width), bf16),
            pltpu.VMEM((CHUNKS, 2, CHUNK, width), bf16),
            pltpu.VMEM((CHUNKS, CHUNK, width // 2), bf16),
            pltpu.VMEM((CHUNKS, CHUNK, width // 2), bf16),
            pltpu.VMEM((CHUNKS, CHUNK, width // 2), f32),
        ]
    return pl.pallas_call(
        kernel,
        out_shape=jax.ShapeDtypeStruct((GRP, 2 * HD), bf16),
        in_specs=[pl.BlockSpec(memory_space=pltpu.HBM)] * len(operands),
        out_specs=pl.BlockSpec(memory_space=pltpu.VMEM),
        scratch_shapes=landing
        + [
            pltpu.VMEM((2, 8, V), bf16),
            pltpu.VMEM((32, V), f32),
            pltpu.VMEM((8, 32, V), bf16),
            pltpu.VMEM((GRP, features), bf16),
            pltpu.VMEM((VIS_GRP, features), bf16),
            pltpu.VMEM((8, 8, TEXT_GRP), f32),
            pltpu.VMEM((8, 8, VIS_GRP), f32),
        ]
        + sums
        + [
            pltpu.VMEM((GRP, HD), f32),
            pltpu.VMEM((GRP, HD), f32),
            pltpu.VMEM((GRP, HD), bf16),
            pltpu.VMEM((GRP, 2 * HD), bf16),
            pltpu.VMEM((GRP, 2 * HD), bf16),
            pltpu.VMEM((NZ, 2, NY, GRP, HD), bf16),
            pltpu.VMEM((2 * GRP, HD), f32),
            pltpu.VMEM((2 * GRP, 2 * HD), f32),
            pltpu.SemaphoreType.DMA((len(operands),)),
            pltpu.SemaphoreType.DMA((AT_SLOTS + 69,)),
            pltpu.SemaphoreType.DMA((AT_SLOTS + 52,)),
        ],
        compiler_params=pltpu.CompilerParams(
            collective_id=0, has_side_effects=True, vmem_limit_bytes=56 * 1024 * 1024
        ),
        name="video_attention",
    )(*operands)


def solution(mesh):
    placed = (
        P("blk", "uly", None),
        P(),
        P(None, "uly"),
        P("blk", "uly"),
        P("blk", None),
        P("uly"),
        P("uly", None),
        P("uly", None),
        P("uly", None),
        P(),
        P(),
        P(),
    )
    return jax.shard_map(
        shards, mesh=mesh, in_specs=placed, out_specs=P("blk", "uly"), check_vma=False
    )
```
